32 devices in a mesh: groups: 2 (over y), wide: 4 (over z), dp: 4 (over x, core).
Axes of the slice: x: 2, y: 2, z: 4, core: 2. Of those that a mesh axis runs over, the one named last changes fastest.
Arguments:
- pair: bfloat16 [8, 256, 256, 128], P(('groups', 'dp'), 'wide'), parts along dimension 0, may hold values from -6 to 6
- lengths: int32 [8], P(('groups', 'dp')), parts along dimension 0, may hold values from 1 to 256, 640 in all
- gain_in: float32 [128], replicated, may hold values from 0.1 to 1.9
- tri_in: bfloat16 [4, 128, 128], replicated, may hold values from -0.5 to 0.5
- tri_gate: bfloat16 [128, 128], replicated, may hold values from -0.5 to 0.5
- gain_mid: float32 [128], replicated, may hold values from 0.1 to 1.9
- tri_out: bfloat16 [128, 128], replicated, may hold values from -0.5 to 0.5
- gain_att: float32 [128], replicated, may hold values from 0.1 to 1.9
- att_in: bfloat16 [4, 128, 128], replicated, may hold values from -0.5 to 0.5
- att_bias: bfloat16 [128, 4], replicated, may hold values from -16 to 16
- att_out: bfloat16 [128, 128], replicated, may hold values from -0.5 to 0.5
Outputs:
- updated_pair: bfloat16 [8, 256, 256, 128], P(('groups', 'dp'), 'wide'), parts along dimension 0
The draws below stay inside these ranges and needn't reach their ends.
There are 2 independent parts, one for each index of `groups`. The reference program is written for one: setup_inputs(seed, part) draws one part's arguments, and reference() takes and returns one part's arrays. A program takes and returns all parts, laid end to end along the dimension named above; an argument that names none is the same for every part. Nothing has to cross between parts.
Inputs may be any that keep to these rules, and one draw needn't show every extreme that they name: `lengths`: each part has a crop of all 256 residues.
All inputs are finite; a program needn't handle non-finite values. No bound on the sum of `lengths` on one device may be relied on, other than what follows from the above.
Results may differ from the reference program's by a relative error of at most 0.023.
Values may be sent and summed in bfloat16 or wider, within the bound.
No kernel may reach another device: no remote copies, remote signals or barrier semaphores. Data moves between devices by JAX's collectives and lax.ppermute only.
A program may use at most 128 MiB of HBM per device.

```python
import math
import jax
import jax.numpy as jnp
import numpy as np
from jax import lax

C = 128
CTRI = 128
HEADS = 4
HEAD_DIM = 32
NRES = 256
HD = 128
CROPS = 4
N_DP = 4


def draw_att_bias(key, part):
    base = jax.random.normal(jax.random.fold_in(key, 11), (C, HEADS), jnp.float32) * (2.5 * C ** (-0.5))
    return jnp.clip(base, -16.0, 16.0).astype(jnp.bfloat16)


def level_of(key, extent, cuts, least, high):
    def one(dim, parts):
        steps = jax.random.uniform(jax.random.fold_in(jax.random.fold_in(key, 6), dim), (parts,), jnp.float32, least / len(cuts), high / len(cuts))
        return jnp.repeat(jnp.exp(steps), extent[dim] // parts).reshape((-1,) + (1,) * (len(extent) - dim - 1))

    level = one(*cuts[0])
    for cut in cuts[1:]:
        level = level * one(*cut)
    return level


def profile(count, total, limit, lean):
    loads = [(1 << 20) // math.isqrt(grade ** lean) + 1 for grade in range(2, count + 1)]
    surplus, holding = total - limit - (count - 1), [1] * (count - 1)
    while surplus > 0:
        free = [i for i in range(count - 1) if holding[i] < limit]
        whole, remaining = sum([loads[i] for i in free]), surplus
        for i in free:
            extra = min(limit - holding[i], max(1, remaining * loads[i] // whole), surplus)
            holding[i] = holding[i] + extra
            surplus = surplus - extra
    return np.array([limit] + holding)


def ragged_sizes(rng, count, total, limit, slope):
    if count == 2:
        one = jax.random.randint(rng, (), max(1, total - limit), min(limit, total - 1) + 1)
        return jnp.stack([one, total - one])
    tallies = jnp.asarray(profile(count, total, limit, slope), jnp.int32)
    couples = (count - 1) // 2
    source_of, taker = tallies[1:1 + 2 * couples:2], tallies[2:2 + 2 * couples:2]
    margin = jnp.minimum(source_of - 1, limit - taker)
    passed = jax.random.randint(jax.random.fold_in(rng, 1), (couples,), 0, 1 << 20) % (margin + 1)
    tallies = tallies.at[1:1 + 2 * couples:2].set(source_of - passed).at[2:2 + 2 * couples:2].set(taker + passed)
    return tallies[jax.random.permutation(jax.random.fold_in(rng, 2), count)]


def centred(own_key, dims, scale, limit, split=(), held_as=jnp.bfloat16):
    entries = scale * jax.random.normal(own_key, dims, jnp.float32)
    if split:
        entries = entries * level_of(own_key, dims, split, -0.22, 0.18)
    return jnp.clip(entries, -limit, limit).astype(held_as)


def setup_inputs(seed: int = 0, part: int = 0) -> dict:
    seeds = jax.random.split(jax.random.key(seed), 12)
    part_splits = jax.random.split(jax.random.fold_in(seeds[11], part), 12)
    return {
        "pair": centred(part_splits[0], (CROPS, NRES, NRES, C), 1.0, 6.0, ((0, 4), (1, 4))),
        "lengths": ragged_sizes(part_splits[1], CROPS, NRES * (N_DP + 1) // 2, NRES, 1).astype(jnp.int32),
        "gain_in": jnp.clip(1.0 + 0.18 * jax.random.normal(seeds[2], (C,), jnp.float32), 0.1, 1.9),
        "tri_in": centred(seeds[3], (4, C, CTRI), C ** -0.5, 0.5),
        "tri_gate": centred(seeds[4], (C, C), C ** -0.5, 0.5),
        "gain_mid": jnp.clip(1.0 + 0.18 * jax.random.normal(seeds[5], (CTRI,), jnp.float32), 0.1, 1.9),
        "tri_out": centred(seeds[6], (CTRI, C), CTRI ** -0.5, 0.5),
        "gain_att": jnp.clip(1.0 + 0.18 * jax.random.normal(seeds[7], (C,), jnp.float32), 0.1, 1.9),
        "att_in": centred(seeds[8], (4, C, HD), C ** -0.5, 0.5),
        "att_bias": draw_att_bias(jax.random.fold_in(seeds[11], 71), part),
        "att_out": centred(seeds[10], (HD, C), HD ** -0.5, 0.5),
    }


def layer_norm(values, gain, axis):
    values = values.astype(jnp.float32)
    center = values - lax.optimization_barrier(jnp.mean(values, axis=axis, keepdims=True))
    spread = lax.optimization_barrier(jnp.mean(center * center, axis=axis, keepdims=True))
    shape = [1] * values.ndim
    shape[axis] = gain.shape[0]
    return center * lax.rsqrt(spread + 1e-05) * gain.reshape(shape).astype(jnp.float32)

def project(normed, weight):
    count = normed.shape[0]
    flat = normed.reshape(count * count, normed.shape[2])
    return jnp.dot(flat, weight, preferred_element_type=jnp.float32).reshape(count, count, weight.shape[1])

def reference(pair, lengths, gain_in, tri_in, tri_gate, gain_mid, tri_out, gain_att, att_in, att_bias, att_out):

    def one_crop(items):
        block, length = items
        count = block.shape[0]
        mask = (jnp.arange(count) < length).astype(jnp.float32)
        pair_mask = (mask[:, None] * mask[None, :])[:, :, None]
        normed = layer_norm(block, gain_in, -1).astype(jnp.bfloat16)
        left = (jax.nn.sigmoid(project(normed, tri_in[0])) * project(normed, tri_in[1]) * pair_mask).astype(jnp.bfloat16)
        right = (jax.nn.sigmoid(project(normed, tri_in[2])) * project(normed, tri_in[3]) * pair_mask).astype(jnp.bfloat16)
        product = jnp.einsum('ikc,jkc->ijc', left.astype(jnp.float32), right.astype(jnp.float32), precision=lax.Precision.HIGHEST).astype(jnp.bfloat16)
        mixed_in = layer_norm(product, gain_mid, -1).astype(jnp.bfloat16)
        gate = jax.nn.sigmoid(project(normed, tri_gate))
        middle = (block.astype(jnp.float32) + gate * project(mixed_in, tri_out)).astype(jnp.bfloat16)
        normed_att = layer_norm(middle, gain_att, -1).astype(jnp.bfloat16)
        queries = jnp.swapaxes(project(normed_att, att_in[0]).astype(jnp.bfloat16), 0, 1)
        keys = jnp.swapaxes(project(normed_att, att_in[1]).astype(jnp.bfloat16), 0, 1)
        values = jnp.swapaxes(project(normed_att, att_in[2]).astype(jnp.bfloat16), 0, 1)
        gates = jnp.swapaxes(jax.nn.sigmoid(project(normed_att, att_in[3])), 0, 1)
        bias = project(normed_att, att_bias).astype(jnp.bfloat16)
        key_bias = jnp.transpose(bias, (2, 1, 0)).astype(jnp.float32) + ((mask - 1.0) * 1000000000.0)[None, None, :]
        scale = HEAD_DIM ** (-0.5)

        def one_column(column):
            query, key, value, gate_col = column
            query = query.reshape(count, HEADS, HEAD_DIM).astype(jnp.float32)
            key = key.reshape(count, HEADS, HEAD_DIM).astype(jnp.float32)
            value = value.reshape(count, HEADS, HEAD_DIM).astype(jnp.float32)
            scores = jnp.einsum('ihd,khd->hik', query, key, precision=lax.Precision.HIGHEST) * scale + key_bias
            weights = jax.nn.softmax(scores, axis=-1).astype(jnp.bfloat16)
            mixed = jnp.einsum('hik,khd->ihd', weights.astype(jnp.float32), value, precision=lax.Precision.HIGHEST).reshape(count, HEADS * HEAD_DIM)
            return (gate_col * mixed).astype(jnp.bfloat16)
        attended = jnp.swapaxes(lax.map(one_column, (queries, keys, values, gates)), 0, 1)
        return (middle.astype(jnp.float32) + project(attended, att_out)).astype(jnp.bfloat16)
    return lax.map(one_crop, (pair, lengths))
```

```python
import functools
import math

import jax
import jax.numpy as jnp
from jax import lax
from jax.experimental import pallas as pl
from jax.experimental.pallas import tpu as pltpu
from jax.sharding import PartitionSpec as P

EPS = 1e-05
BLOCK = 16
LANES = 128
LOG2E = math.log2(math.e)
VMEM = 40 * 1024 * 1024
F32 = jnp.float32
BF16 = jnp.bfloat16
NT = (((1,), (1,)), ((), ()))


def layer_norm(values, gain, axis):
    values = values.astype(jnp.float32)
    center = values - jnp.mean(values, axis=axis, keepdims=True)
    spread = jnp.mean(center * center, axis=axis, keepdims=True)
    shape = [1] * values.ndim
    shape[axis] = gain.shape[0]
    return center * lax.rsqrt(spread + EPS) * gain.reshape(shape)


def edge_operand(normed, weights, gate_index, proj_index, pair_mask):
    gate = jnp.einsum(
        "ikd,de->eik", normed, weights[gate_index], preferred_element_type=jnp.float32
    )
    proj = jnp.einsum(
        "ikd,de->eik", normed, weights[proj_index], preferred_element_type=jnp.float32
    )
    return (jax.nn.sigmoid(gate) * proj * pair_mask[None]).astype(jnp.bfloat16)


def row_update(block, normed, product, gain_mid, tri_out, tri_gate, gain_att, att_bias):
    mixed_in = layer_norm(product, gain_mid, 0).astype(jnp.bfloat16)
    update = jnp.einsum("cij,cd->ijd", mixed_in, tri_out, preferred_element_type=jnp.float32)
    gate = jax.nn.sigmoid(
        jnp.einsum("ijd,de->ije", normed, tri_gate, preferred_element_type=jnp.float32)
    )
    middle_rows = (block.astype(jnp.float32) + gate * update).astype(jnp.bfloat16)
    normed_rows = layer_norm(middle_rows, gain_att, 2).astype(jnp.bfloat16)
    bias_part = jnp.einsum(
        "ijc,ch->hij", normed_rows, att_bias, preferred_element_type=jnp.float32
    ).astype(jnp.bfloat16)
    return (middle_rows, bias_part)


def column_attention(normed, att_in, key_bias, heads):
    queries = jnp.einsum(
        "ijc,ce->jie", normed, att_in[0], preferred_element_type=jnp.float32
    ).astype(jnp.bfloat16)
    keys = jnp.einsum("ijc,ce->jie", normed, att_in[1], preferred_element_type=jnp.float32).astype(
        jnp.bfloat16
    )
    values = jnp.einsum(
        "ijc,ce->jie", normed, att_in[2], preferred_element_type=jnp.float32
    ).astype(jnp.bfloat16)
    gates = jax.nn.sigmoid(
        jnp.einsum("ijc,ce->jie", normed, att_in[3], preferred_element_type=jnp.float32)
    )
    count = queries.shape[1]
    width_all = queries.shape[2]
    depth = width_all // heads
    scale = depth ** (-0.5)

    def one_column(column):
        query, key, value, gate_col = column
        query = query.reshape(count, heads, depth)
        key = key.reshape(count, heads, depth)
        value = value.reshape(count, heads, depth)
        scores = (
            jnp.einsum("ihd,khd->hik", query, key, preferred_element_type=jnp.float32) * scale
            + key_bias
        )
        weights = jax.nn.softmax(scores, axis=-1).astype(jnp.bfloat16)
        mixed = jnp.einsum(
            "hik,khd->ihd", weights, value, preferred_element_type=jnp.float32
        ).reshape(count, width_all)
        return (gate_col * mixed).astype(jnp.bfloat16)

    return lax.map(one_column, (queries, keys, values, gates))


def general_body(
    pair, lengths, gain_in, tri_in, tri_gate, gain_mid, tri_out, gain_att, att_in, att_bias, att_out
):
    block = pair[0]
    rows = block.shape[0]
    count = block.shape[1]
    heads = att_bias.shape[1]
    first = lax.axis_index("wide") * rows
    mask = (jnp.arange(count) < lengths[0]).astype(jnp.float32)
    row_mask = lax.dynamic_slice_in_dim(mask, first, rows)
    pair_mask = row_mask[:, None] * mask[None, :]
    normed = layer_norm(block, gain_in, 2).astype(jnp.bfloat16)
    left = edge_operand(normed, tri_in, 0, 1, pair_mask)
    right = edge_operand(normed, tri_in, 2, 3, pair_mask)
    key_mask = ((mask - 1.0) * 1000000000.0)[None, None, :]
    left_ch, right_ch = (
        lax.all_to_all(left, "wide", split_axis=0, concat_axis=1, tiled=True),
        lax.all_to_all(right, "wide", split_axis=0, concat_axis=1, tiled=True),
    )
    product = jnp.einsum(
        "cik,cjk->cij", left_ch, right_ch, preferred_element_type=jnp.float32
    ).astype(jnp.bfloat16)
    product = lax.all_to_all(product, "wide", split_axis=1, concat_axis=0, tiled=True)
    middle_rows, bias_part = row_update(
        block, normed, product, gain_mid, tri_out, tri_gate, gain_att, att_bias
    )
    middle = lax.all_to_all(middle_rows, "wide", split_axis=1, concat_axis=0, tiled=True)
    table = lax.all_gather(bias_part, "wide", axis=1, tiled=True)
    normed_att = layer_norm(middle, gain_att, 2).astype(jnp.bfloat16)
    key_bias = jnp.swapaxes(table, 1, 2).astype(jnp.float32) + key_mask
    attended = column_attention(normed_att, att_in, key_bias, heads)
    result = jnp.einsum("jie,ec->ijc", attended, att_out, preferred_element_type=jnp.float32)
    finished = (middle.astype(jnp.float32) + result).astype(jnp.bfloat16)
    back = lax.all_to_all(finished, "wide", split_axis=0, concat_axis=1, tiled=True)
    return back[None]


def norm_rows(values, ones, gain):
    mean = jnp.dot(values.astype(BF16), ones, preferred_element_type=F32)
    center = values - mean
    spread = jnp.dot((center * center).astype(BF16), ones, preferred_element_type=F32)
    return (center * lax.rsqrt(spread + EPS) * gain).astype(BF16)


def operand_kernel(sides, first_index, scalars, x_ref, gain_ref, weight_ref, *refs):
    outs, works = refs[:sides], refs[sides:]
    count, chan = x_ref.shape[1], x_ref.shape[2]
    length = scalars[0]
    row0 = scalars[first_index] + pl.program_id(0) * BLOCK
    ones = jnp.full((chan, chan), 1.0 / chan, BF16)
    key_mask = (lax.broadcasted_iota(jnp.int32, (1, count), 1) < length).astype(F32)

    def step(r, carry):
        normed = norm_rows(x_ref[r].astype(F32), ones, gain_ref[...])
        row_mask = key_mask * (row0 + r < length).astype(F32)
        for side in range(sides):
            gate = lax.dot_general(weight_ref[2 * side], normed, NT, preferred_element_type=F32)
            proj = lax.dot_general(weight_ref[2 * side + 1], normed, NT, preferred_element_type=F32)
            value = (jnp.tanh(gate) + 1.0) * proj * row_mask
            for lane in range(count // LANES):
                works[side][lane, pl.ds(r, chan, stride=BLOCK), :] = value[
                    :, lane * LANES : (lane + 1) * LANES
                ]
        return carry

    lax.fori_loop(0, BLOCK, step, 0, unroll=2)
    for side in range(sides):
        for lane in range(count // LANES):
            outs[side][:, :, lane * LANES : (lane + 1) * LANES] = (
                works[side][lane].reshape(chan, BLOCK, LANES).astype(BF16)
            )


def operands(x, scalars, first_index, gain, weights, sides):
    rows, count, chan = x.shape
    out = jax.ShapeDtypeStruct((chan, rows, count), BF16)
    return pl.pallas_call(
        functools.partial(operand_kernel, sides, first_index),
        grid_spec=pltpu.PrefetchScalarGridSpec(
            num_scalar_prefetch=1,
            grid=(rows // BLOCK,),
            in_specs=[
                pl.BlockSpec((BLOCK, count, chan), lambda i, s: (i, 0, 0)),
                pl.BlockSpec((1, chan), lambda i, s: (0, 0)),
                pl.BlockSpec((2 * sides, chan, chan), lambda i, s: (0, 0, 0)),
            ],
            out_specs=[pl.BlockSpec((chan, BLOCK, count), lambda i, s: (0, i, 0))] * sides,
            scratch_shapes=[pltpu.VMEM((count // LANES, chan * BLOCK, LANES), F32)] * sides,
        ),
        out_shape=[out] * sides,
        compiler_params=pltpu.CompilerParams(vmem_limit_bytes=VMEM),
        cost_estimate=pl.CostEstimate(
            flops=2 * rows * count * chan * chan * (2 + 2 * sides),
            bytes_accessed=2 * rows * count * chan * (1 + sides),
            transcendentals=rows * count * chan * sides,
        ),
    )(scalars, x, gain, weights[: 2 * sides])


def product_kernel(left_ref, mine_ref, partner_ref, out_ref):
    for c in range(left_ref.shape[0]):
        right = jnp.concatenate([mine_ref[c], partner_ref[c]], axis=0)
        out_ref[c] = lax.dot_general(left_ref[c], right, NT, preferred_element_type=F32).astype(BF16)


def products(left, mine, partner):
    chan, rows, count = left.shape
    own = mine.shape[1]
    step = 8
    return pl.pallas_call(
        product_kernel,
        grid=(chan // step,),
        in_specs=[
            pl.BlockSpec((step, rows, count), lambda i: (i, 0, 0)),
            pl.BlockSpec((step, own, count), lambda i: (i, 0, 0)),
            pl.BlockSpec((step, own, count), lambda i: (i, 0, 0)),
        ],
        out_specs=pl.BlockSpec((step, rows, 2 * own), lambda i: (i, 0, 0)),
        out_shape=jax.ShapeDtypeStruct((chan, rows, 2 * own), BF16),
        compiler_params=pltpu.CompilerParams(vmem_limit_bytes=VMEM),
        cost_estimate=pl.CostEstimate(
            flops=2 * chan * rows * count * 2 * own,
            bytes_accessed=2 * chan * (rows * count + 2 * own * count + rows * 2 * own),
            transcendentals=0,
        ),
    )(left, mine, partner)


def update_kernel(
    scalars,
    prod_ref,
    xm_ref,
    xp_ref,
    gain_in_ref,
    gain_mid_ref,
    gain_att_ref,
    out_w_ref,
    gate_w_ref,
    bias_w_ref,
    mine_ref,
    partner_ref,
    bias_ref,
    work,
    bias_work,
):
    chan, _, wide = prod_ref.shape
    own = wide // 2
    heads = bias_ref.shape[0]
    pad = bias_w_ref.shape[0]
    ones = jnp.full((chan, chan), 1.0 / chan, BF16)
    work[...] = prod_ref[...].astype(F32).reshape(chan * BLOCK, wide)

    def step(r, carry):
        prod = work[pl.ds(r, chan, stride=BLOCK), :]
        center = prod - jnp.mean(prod, axis=0, keepdims=True)
        spread = jnp.mean(center * center, axis=0, keepdims=True)
        mixed = (center * lax.rsqrt(spread + EPS) * gain_mid_ref[...]).astype(BF16)
        update = jnp.dot(out_w_ref[...], mixed, preferred_element_type=F32).T
        x = jnp.concatenate([xm_ref[r], xp_ref[r]], axis=0).astype(F32)
        normed = norm_rows(x, ones, gain_in_ref[...])
        gate = jnp.tanh(jnp.dot(normed, gate_w_ref[...], preferred_element_type=F32)) + 1.0
        middle = (x + gate * update).astype(BF16)
        mine_ref[r] = middle[:own]
        partner_ref[r] = middle[own:]
        normed_att = norm_rows(middle.astype(F32), ones, gain_att_ref[...])
        bias_work[pl.ds(r, pad, stride=BLOCK), :] = lax.dot_general(
            bias_w_ref[...], normed_att, NT, preferred_element_type=F32
        )
        return carry

    lax.fori_loop(0, BLOCK, step, 0, unroll=2)
    bias_ref[...] = bias_work[: heads * BLOCK, :].reshape(heads, BLOCK, wide).astype(BF16)


def updates(prod, x, scalars, gain_in, gain_mid, gain_att, out_w, gate_w, bias_w, heads):
    chan, rows, wide = prod.shape
    own = wide // 2
    pad = bias_w.shape[0]
    full = lambda *shape: pl.BlockSpec(shape, lambda i, s: (0,) * len(shape))
    return pl.pallas_call(
        update_kernel,
        grid_spec=pltpu.PrefetchScalarGridSpec(
            num_scalar_prefetch=1,
            grid=(rows // BLOCK,),
            in_specs=[
                pl.BlockSpec((chan, BLOCK, wide), lambda i, s: (0, i, 0)),
                pl.BlockSpec((BLOCK, own, chan), lambda i, s: (i, s[1], 0)),
                pl.BlockSpec((BLOCK, own, chan), lambda i, s: (i, s[2], 0)),
                full(1, chan),
                full(chan, 1),
                full(1, chan),
                full(chan, chan),
                full(chan, chan),
                full(pad, chan),
            ],
            out_specs=[
                pl.BlockSpec((BLOCK, own, chan), lambda i, s: (i, 0, 0)),
                pl.BlockSpec((BLOCK, own, chan), lambda i, s: (i, 0, 0)),
                pl.BlockSpec((heads, BLOCK, wide), lambda i, s: (0, i, 0)),
            ],
            scratch_shapes=[
                pltpu.VMEM((chan * BLOCK, wide), F32),
                pltpu.VMEM((pad * BLOCK, wide), F32),
            ],
        ),
        out_shape=[
            jax.ShapeDtypeStruct((rows, own, chan), BF16),
            jax.ShapeDtypeStruct((rows, own, chan), BF16),
            jax.ShapeDtypeStruct((heads, rows, wide), BF16),
        ],
        compiler_params=pltpu.CompilerParams(vmem_limit_bytes=VMEM),
        cost_estimate=pl.CostEstimate(
            flops=2 * rows * wide * chan * chan * 7,
            bytes_accessed=2 * rows * wide * chan * 3,
            transcendentals=rows * wide * chan * 3,
        ),
    )(scalars, prod, x, x, gain_in, gain_mid, gain_att, out_w, gate_w, bias_w)


def attention_kernel(
    parts, heads, scalars, bias_own_ref, bias_oth_ref, gain_ref, wk_ref, wt_ref, wo_ref, *refs
):
    mine, recv = refs[:parts], refs[parts : 2 * parts]
    outs = refs[2 * parts : 2 * parts + 4]
    table, work, result = refs[2 * parts + 4 :]
    count = table.shape[1]
    chan = work.shape[1]
    own = outs[0].shape[0]
    depth = chan // heads
    length = scalars[0]
    ones = jnp.full((chan, chan), 1.0 / chan, BF16)
    half = count // 2

    @pl.when(scalars[11] == 0)
    def _():
        first = 0
        for ref in mine:
            size = ref.shape[0] * BLOCK
            work[first : first + size, :] = ref[...].astype(F32).reshape(size, chan)
            first += size

    @pl.when(scalars[11] != 0)
    def _():
        first = 0
        for ref in recv:
            size = ref.shape[0] * BLOCK
            work[first : first + size, :] = ref[...].astype(F32).reshape(size, chan)
            first += size

    for part in range(4):
        place = lax.broadcasted_iota(jnp.int32, (own, half), 0) + scalars[3 + part] * own
        masked = (jnp.where(place < length, 1.0, 0.0) - 1.0) * (1e9 * LOG2E)
        turned = (part + 2) % 4
        for h in range(heads):
            rows = pl.ds(part * own, own)
            table[h, rows, :half] = bias_own_ref[h, rows, :].astype(F32) * LOG2E + masked
            table[h, rows, half:] = (
                bias_oth_ref[h, pl.ds(turned * own, own), :].astype(F32) * LOG2E + masked
            )

    def column(b, carry):
        x = work[pl.ds(b, count, stride=BLOCK), :]
        normed = norm_rows(x, ones, gain_ref[...])
        keys = jnp.dot(normed, wk_ref[...], preferred_element_type=F32).astype(BF16)
        query = lax.dot_general(wt_ref[0], normed, NT, preferred_element_type=F32)
        query = (query * (depth ** (-0.5) * LOG2E)).astype(BF16)
        value = lax.dot_general(wt_ref[1], normed, NT, preferred_element_type=F32).astype(BF16)
        gate = jnp.tanh(lax.dot_general(wt_ref[2], normed, NT, preferred_element_type=F32))
        gate = 0.5 * gate + 0.5
        attended = []
        for h in range(heads):
            pieces = []
            if h > 0:
                pieces.append(jnp.zeros((h * depth, count), BF16))
            pieces.append(query[h * depth : (h + 1) * depth])
            if h < heads - 1:
                pieces.append(jnp.zeros(((heads - 1 - h) * depth, count), BF16))
            alone = jnp.concatenate(pieces, axis=0)
            scores = jnp.dot(keys, alone, preferred_element_type=F32) + table[h]
            weights = jnp.exp2(scores - jnp.max(scores, axis=0, keepdims=True))
            total = jnp.sum(weights, axis=0, keepdims=True)
            mixed = jnp.dot(
                value[h * depth : (h + 1) * depth],
                weights.astype(BF16),
                preferred_element_type=F32,
            )
            attended.append(mixed * (1.0 / total) * gate[h * depth : (h + 1) * depth])
        attended = jnp.concatenate(attended, axis=0).astype(BF16)
        update = jnp.dot(wo_ref[...], attended, preferred_element_type=F32).T
        result[pl.ds(b, count, stride=BLOCK), :] = x + update
        return carry

    lax.fori_loop(0, BLOCK, column, 0)
    for d in range(4):
        rows = pl.ds(pl.multiple_of(scalars[7 + d] * (own * BLOCK), own * BLOCK), own * BLOCK)
        outs[d][...] = result[rows, :].reshape(own, BLOCK, chan).astype(BF16)


def attention(index, scalars, bias_own, bias_oth, gain, wk, wt, wo, mine, recv, heads):
    own, chan = mine[0].shape[1], mine[0].shape[2]
    count = 4 * own
    full = lambda *shape: pl.BlockSpec(shape, lambda i, s: (0,) * len(shape))
    pieces = [pl.BlockSpec((m.shape[0], BLOCK, chan), lambda i, s: (0, index, 0)) for m in mine]
    return pl.pallas_call(
        functools.partial(attention_kernel, len(mine), heads),
        grid_spec=pltpu.PrefetchScalarGridSpec(
            num_scalar_prefetch=1,
            grid=(1,),
            in_specs=[
                full(heads, count, count // 2),
                full(heads, count, count // 2),
                full(1, chan),
                full(chan, chan),
                full(3, chan, chan),
                full(chan, chan),
            ]
            + pieces
            + pieces,
            out_specs=[full(own, BLOCK, chan)] * 4,
            scratch_shapes=[
                pltpu.VMEM((heads, count, count), F32),
                pltpu.VMEM((count * BLOCK, chan), F32),
                pltpu.VMEM((count * BLOCK, chan), F32),
            ],
        ),
        out_shape=[jax.ShapeDtypeStruct((own, BLOCK, chan), BF16)] * 4,
        compiler_params=pltpu.CompilerParams(vmem_limit_bytes=VMEM),
        cost_estimate=pl.CostEstimate(
            flops=2 * BLOCK * (count * chan * chan * 7 + 2 * heads * count * count * chan),
            bytes_accessed=2 * count * BLOCK * chan * 3,
            transcendentals=BLOCK * heads * count * count,
        ),
    )(scalars, bias_own, bias_oth, gain, wk, wt, wo, *mine, *recv)


def line_body(
    pair, lengths, gain_in, tri_in, tri_gate, gain_mid, tri_out, gain_att, att_in, att_bias, att_out
):
    own_rows = pair[0]
    own, count, chan = own_rows.shape
    heads = att_bias.shape[1]
    z = lax.axis_index("wide")
    inner = jnp.where(z < 2, 1, 2)
    partner = inner ^ 1
    other_in = 3 - inner
    other_out = other_in ^ 1
    order = jnp.stack([inner, partner, other_in, other_out])
    outer = ((z == 0) | (z == 3)).astype(jnp.int32)
    place = jnp.stack([jnp.argmax(order == (z + d) % 4) for d in range(4)])
    half_rows = own // 2
    firsts = order * own
    scalars = jnp.concatenate(
        [
            lengths[:1],
            jnp.stack([inner, partner]),
            order,
            place,
            jnp.stack([outer]),
            firsts,
            firsts + half_rows,
        ]
    ).astype(jnp.int32)

    to_inner = [(0, 1), (3, 2)]
    to_outer = [(1, 0), (2, 3)]
    middle_link = [(1, 2), (2, 1)]
    send = lambda v, pairs: lax.ppermute(v, "wide", pairs)

    partner_parts = [send(own_rows[:half_rows], to_inner), send(own_rows[half_rows:], to_inner)]
    rows_oi = send(own_rows, middle_link)
    rows_oo = [send(v, middle_link) for v in partner_parts]

    tri_w = (jnp.swapaxes(tri_in, 1, 2).astype(F32) * 0.5).astype(BF16)
    gain_row = gain_in.reshape(1, chan)
    left_own, right_own = operands(own_rows, scalars, 12, gain_row, tri_w, 2)
    chunks = [(own_rows, left_own)]
    rights = []
    rows_p = jnp.concatenate(partner_parts, axis=0)
    left_p, right_p = operands(rows_p, scalars, 13, gain_row, tri_w, 2)
    chunks.append((rows_p, left_p))
    chunks.append((rows_oi, operands(rows_oi, scalars, 14, gain_row, tri_w, 1)[0]))
    chunks.append((rows_oo[0], operands(rows_oo[0], scalars, 15, gain_row, tri_w, 1)[0]))
    chunks.append((rows_oo[1], operands(rows_oo[1], scalars, 19, gain_row, tri_w, 1)[0]))

    out_w = (tri_out.astype(F32) * 0.5).astype(BF16).T
    gate_w = (tri_gate.astype(F32) * 0.5).astype(BF16)
    bias_w = jnp.zeros((8, chan), BF16).at[:heads].set(att_bias.T)
    mine, recv, biases = [], [], []
    for rows, left in chunks:
        prod = products(left, right_own, right_p)
        kept, sent, bias = updates(
            prod,
            rows,
            scalars,
            gain_row,
            gain_mid.reshape(chan, 1),
            gain_att.reshape(1, chan),
            out_w,
            gate_w,
            bias_w,
            heads,
        )
        mine.append(kept)
        recv.append(send(sent, to_outer))
        biases.append(bias)

    bias_own = jnp.concatenate(biases, axis=1)
    bias_oth = send(bias_own, middle_link)
    got_own, got_oth = send(bias_own, to_outer), send(bias_oth, to_outer)
    bias_own = jnp.where(outer == 1, got_own, bias_own)
    bias_oth = jnp.where(outer == 1, got_oth, bias_oth)

    att_t = jnp.swapaxes(att_in, 1, 2)
    wt = jnp.stack([att_t[0], att_t[2], (att_t[3].astype(F32) * 0.5).astype(BF16)])
    output = jnp.zeros((own, count, chan), BF16)
    for index in range(own // BLOCK):
        outs = attention(
            index,
            scalars,
            bias_own,
            bias_oth,
            gain_att.reshape(1, chan),
            att_in[1],
            wt,
            att_out.T,
            mine,
            recv,
            heads,
        )
        for d in range(4):
            piece = outs[d]
            if d > 0:
                piece = send(piece, [(i, (i + d) % 4) for i in range(4)])
            source = (z - d) % 4
            output = lax.dynamic_update_slice(output, piece, (0, source * own + index * BLOCK, 0))
    return output[None]


def solution(mesh):
    in_specs = (
        P(("groups", "dp"), "wide", None, None),
        P(("groups", "dp")),
        P(),
        P(),
        P(),
        P(),
        P(),
        P(),
        P(),
        P(),
        P(),
    )
    out_specs = P(("groups", "dp"), "wide", None, None)
    body = line_body if mesh.shape["wide"] == 4 else general_body
    return jax.shard_map(body, mesh=mesh, in_specs=in_specs, out_specs=out_specs, check_vma=False)
```

```python
import functools
import math

import jax
import jax.numpy as jnp
from jax import lax
from jax.experimental import pallas as pl
from jax.experimental.pallas import tpu as pltpu
from jax.sharding import PartitionSpec as P

EPS = 1e-05
BLOCK = 16
LANES = 128
LOG2E = math.log2(math.e)
VMEM = 40 * 1024 * 1024
F32 = jnp.float32
BF16 = jnp.bfloat16
NT = (((1,), (1,)), ((), ()))


def layer_norm(values, gain, axis):
    values = values.astype(jnp.float32)
    center = values - jnp.mean(values, axis=axis, keepdims=True)
    spread = jnp.mean(center * center, axis=axis, keepdims=True)
    shape = [1] * values.ndim
    shape[axis] = gain.shape[0]
    return center * lax.rsqrt(spread + EPS) * gain.reshape(shape)


def edge_operand(normed, weights, gate_index, proj_index, pair_mask):
    gate = jnp.einsum(
        "ikd,de->eik", normed, weights[gate_index], preferred_element_type=jnp.float32
    )
    proj = jnp.einsum(
        "ikd,de->eik", normed, weights[proj_index], preferred_element_type=jnp.float32
    )
    return (jax.nn.sigmoid(gate) * proj * pair_mask[None]).astype(jnp.bfloat16)


def row_update(block, normed, product, gain_mid, tri_out, tri_gate, gain_att, att_bias):
    mixed_in = layer_norm(product, gain_mid, 0).astype(jnp.bfloat16)
    update = jnp.einsum("cij,cd->ijd", mixed_in, tri_out, preferred_element_type=jnp.float32)
    gate = jax.nn.sigmoid(
        jnp.einsum("ijd,de->ije", normed, tri_gate, preferred_element_type=jnp.float32)
    )
    middle_rows = (block.astype(jnp.float32) + gate * update).astype(jnp.bfloat16)
    normed_rows = layer_norm(middle_rows, gain_att, 2).astype(jnp.bfloat16)
    bias_part = jnp.einsum(
        "ijc,ch->hij", normed_rows, att_bias, preferred_element_type=jnp.float32
    ).astype(jnp.bfloat16)
    return (middle_rows, bias_part)


def column_attention(normed, att_in, key_bias, heads):
    queries = jnp.einsum(
        "ijc,ce->jie", normed, att_in[0], preferred_element_type=jnp.float32
    ).astype(jnp.bfloat16)
    keys = jnp.einsum("ijc,ce->jie", normed, att_in[1], preferred_element_type=jnp.float32).astype(
        jnp.bfloat16
    )
    values = jnp.einsum(
        "ijc,ce->jie", normed, att_in[2], preferred_element_type=jnp.float32
    ).astype(jnp.bfloat16)
    gates = jax.nn.sigmoid(
        jnp.einsum("ijc,ce->jie", normed, att_in[3], preferred_element_type=jnp.float32)
    )
    count = queries.shape[1]
    width_all = queries.shape[2]
    depth = width_all // heads
    scale = depth ** (-0.5)

    def one_column(column):
        query, key, value, gate_col = column
        query = query.reshape(count, heads, depth)
        key = key.reshape(count, heads, depth)
        value = value.reshape(count, heads, depth)
        scores = (
            jnp.einsum("ihd,khd->hik", query, key, preferred_element_type=jnp.float32) * scale
            + key_bias
        )
        weights = jax.nn.softmax(scores, axis=-1).astype(jnp.bfloat16)
        mixed = jnp.einsum(
            "hik,khd->ihd", weights, value, preferred_element_type=jnp.float32
        ).reshape(count, width_all)
        return (gate_col * mixed).astype(jnp.bfloat16)

    return lax.map(one_column, (queries, keys, values, gates))


def general_body(
    pair, lengths, gain_in, tri_in, tri_gate, gain_mid, tri_out, gain_att, att_in, att_bias, att_out
):
    block = pair[0]
    rows = block.shape[0]
    count = block.shape[1]
    heads = att_bias.shape[1]
    first = lax.axis_index("wide") * rows
    mask = (jnp.arange(count) < lengths[0]).astype(jnp.float32)
    row_mask = lax.dynamic_slice_in_dim(mask, first, rows)
    pair_mask = row_mask[:, None] * mask[None, :]
    normed = layer_norm(block, gain_in, 2).astype(jnp.bfloat16)
    left = edge_operand(normed, tri_in, 0, 1, pair_mask)
    right = edge_operand(normed, tri_in, 2, 3, pair_mask)
    key_mask = ((mask - 1.0) * 1000000000.0)[None, None, :]
    left_ch, right_ch = (
        lax.all_to_all(left, "wide", split_axis=0, concat_axis=1, tiled=True),
        lax.all_to_all(right, "wide", split_axis=0, concat_axis=1, tiled=True),
    )
    product = jnp.einsum(
        "cik,cjk->cij", left_ch, right_ch, preferred_element_type=jnp.float32
    ).astype(jnp.bfloat16)
    product = lax.all_to_all(product, "wide", split_axis=1, concat_axis=0, tiled=True)
    middle_rows, bias_part = row_update(
        block, normed, product, gain_mid, tri_out, tri_gate, gain_att, att_bias
    )
    middle = lax.all_to_all(middle_rows, "wide", split_axis=1, concat_axis=0, tiled=True)
    table = lax.all_gather(bias_part, "wide", axis=1, tiled=True)
    normed_att = layer_norm(middle, gain_att, 2).astype(jnp.bfloat16)
    key_bias = jnp.swapaxes(table, 1, 2).astype(jnp.float32) + key_mask
    attended = column_attention(normed_att, att_in, key_bias, heads)
    result = jnp.einsum("jie,ec->ijc", attended, att_out, preferred_element_type=jnp.float32)
    finished = (middle.astype(jnp.float32) + result).astype(jnp.bfloat16)
    back = lax.all_to_all(finished, "wide", split_axis=0, concat_axis=1, tiled=True)
    return back[None]


def norm_columns(values, gain):
    center = values - jnp.mean(values, axis=0, keepdims=True)
    spread = jnp.mean(center * center, axis=0, keepdims=True)
    return (center * lax.rsqrt(spread + EPS) * gain).astype(BF16)


def full_block(*shape):
    return pl.BlockSpec(shape, lambda i, s: (0,) * len(shape))


def operand_kernel(sides, first_index, scalars, x_ref, gain_ref, weight_ref, *refs):
    outs, works = refs[:sides], refs[sides:]
    count, chan = x_ref.shape[1], x_ref.shape[2]
    length = scalars[0]
    row0 = scalars[first_index] + pl.program_id(0) * BLOCK
    key_mask = (lax.broadcasted_iota(jnp.int32, (1, count), 1) < length).astype(F32)

    def step(r, carry):
        normed = norm_columns(x_ref[r].astype(F32).T, gain_ref[...])
        both = jnp.dot(weight_ref[...], normed, preferred_element_type=F32)
        row_mask = key_mask * (row0 + r < length).astype(F32)
        for side in range(sides):
            gate = both[2 * side * chan : (2 * side + 1) * chan]
            proj = both[(2 * side + 1) * chan : (2 * side + 2) * chan]
            value = (jnp.tanh(gate) + 1.0) * proj * row_mask
            for lane in range(count // LANES):
                works[side][lane, pl.ds(r, chan, stride=BLOCK), :] = value[
                    :, lane * LANES : (lane + 1) * LANES
                ]
        return carry

    lax.fori_loop(0, BLOCK, step, 0, unroll=8)
    for side in range(sides):
        for lane in range(count // LANES):
            outs[side][:, :, lane * LANES : (lane + 1) * LANES] = (
                works[side][lane].reshape(chan, BLOCK, LANES).astype(BF16)
            )


def operands(x, scalars, first_index, gain, weights, sides):
    rows, count, chan = x.shape
    out = jax.ShapeDtypeStruct((chan, rows, count), BF16)
    return pl.pallas_call(
        functools.partial(operand_kernel, sides, first_index),
        grid_spec=pltpu.PrefetchScalarGridSpec(
            num_scalar_prefetch=1,
            grid=(rows // BLOCK,),
            in_specs=[
                pl.BlockSpec((BLOCK, count, chan), lambda i, s: (i, 0, 0)),
                full_block(chan, 1),
                full_block(2 * sides * chan, chan),
            ],
            out_specs=[pl.BlockSpec((chan, BLOCK, count), lambda i, s: (0, i, 0))] * sides,
            scratch_shapes=[pltpu.VMEM((count // LANES, chan * BLOCK, LANES), F32)] * sides,
        ),
        out_shape=[out] * sides,
        compiler_params=pltpu.CompilerParams(vmem_limit_bytes=VMEM),
        cost_estimate=pl.CostEstimate(
            flops=2 * rows * count * chan * chan * (2 + 2 * sides),
            bytes_accessed=2 * rows * count * chan * (1 + sides),
            transcendentals=rows * count * chan * sides,
        ),
    )(scalars, x, gain, weights[: 2 * sides * chan])


def product_kernel(lefts, *refs):
    left_refs, (mine_ref, *partner_refs) = refs[:lefts], refs[lefts:-2]
    own_ref, out_ref = refs[-2:]
    half, own = own_ref.shape[1], mine_ref.shape[1]
    for c in range(own_ref.shape[0]):
        left = [ref[c] for ref in left_refs]
        left = left[0] if lefts == 1 else jnp.concatenate(left, axis=0)
        right = jnp.concatenate([mine_ref[c]] + [ref[c] for ref in partner_refs], axis=0)
        prod = lax.dot_general(left, right, NT, preferred_element_type=F32)
        low, high = prod[:half], prod[half:]
        own_ref[c] = jnp.concatenate([low[:, :own], high[:, :own]], axis=1).astype(BF16)
        out_ref[c] = jnp.concatenate([low[:, own:], high[:, own:]], axis=1).astype(BF16)


def products(lefts, rights):
    chan, count = lefts[0].shape[0], lefts[0].shape[2]
    rows = sum(v.shape[1] for v in lefts)
    own = rights[0].shape[1]
    step = 16
    spec = lambda v: pl.BlockSpec((step,) + v.shape[1:], lambda i: (i, 0, 0))
    out = jax.ShapeDtypeStruct((chan, rows // 2, 2 * own), BF16)
    return pl.pallas_call(
        functools.partial(product_kernel, len(lefts)),
        grid=(chan // step,),
        in_specs=[spec(v) for v in lefts + rights],
        out_specs=[spec(out), spec(out)],
        out_shape=[out, out],
        compiler_params=pltpu.CompilerParams(vmem_limit_bytes=VMEM),
        cost_estimate=pl.CostEstimate(
            flops=2 * chan * rows * count * 2 * own,
            bytes_accessed=2 * chan * (rows * count + 2 * own * count + rows * 2 * own),
            transcendentals=0,
        ),
    )(*lefts, *rights)


def update_kernel(
    scalars,
    prod_ref,
    prod_got_ref,
    low_ref,
    high_ref,
    low_got_ref,
    high_got_ref,
    gain_in_ref,
    gain_mid_ref,
    gain_att_ref,
    out_w_ref,
    gate_w_ref,
    bias_w_ref,
    low_out,
    high_out,
    bias_ref,
    work,
    bias_work,
    normed_work,
    mixed_work,
    x_work,
):
    chan, _, wide = prod_ref.shape
    heads = bias_ref.shape[0]
    pad = bias_w_ref.shape[0]
    own = wide // 2
    outer = scalars[11] != 0

    @pl.when(outer)
    def _():
        work[...] = prod_got_ref[...].astype(F32).reshape(chan * BLOCK, wide)

    @pl.when(jnp.logical_not(outer))
    def _():
        work[...] = prod_ref[...].astype(F32).reshape(chan * BLOCK, wide)

    def load(r, carry):
        lane = pl.ds(pl.multiple_of(r * wide, wide), wide)
        mixed_work[:, lane] = norm_columns(work[pl.ds(r, chan, stride=BLOCK), :], gain_mid_ref[...])
        low = jnp.where(outer, low_got_ref[r], low_ref[r])
        high = jnp.where(outer, high_got_ref[r], high_ref[r])
        x = jnp.concatenate([low, high], axis=0).astype(F32).T
        x_work[:, lane] = x
        normed_work[:, lane] = norm_columns(x, gain_in_ref[...])
        return carry

    lax.fori_loop(0, BLOCK, load, 0, unroll=4)
    group = 8

    def update(j, carry):
        lane = pl.ds(pl.multiple_of(j * group * wide, group * wide), group * wide)
        gate = jnp.tanh(jnp.dot(gate_w_ref[...], normed_work[:, lane], preferred_element_type=F32))
        change = jnp.dot(out_w_ref[...], mixed_work[:, lane], preferred_element_type=F32)
        middle = (x_work[:, lane] + (gate + 1.0) * change).astype(BF16).astype(F32)
        normed_att = norm_columns(middle, gain_att_ref[...])
        bias = jnp.dot(bias_w_ref[...], normed_att, preferred_element_type=F32)
        for i in range(group):
            r = j * group + i
            turned = middle[:, i * wide : (i + 1) * wide].T.astype(BF16)
            low_out[r] = turned[:own]
            high_out[r] = turned[own:]
            bias_work[pl.ds(r, pad, stride=BLOCK), :] = bias[:, i * wide : (i + 1) * wide]
        return carry

    lax.fori_loop(0, BLOCK // group, update, 0)
    bias_ref[...] = bias_work[: heads * BLOCK, :].reshape(heads, BLOCK, wide).astype(BF16)


def updates(prod, prod_got, low, high, low_got, high_got, scalars, small, heads):
    chan, half, wide = prod.shape
    own = wide // 2

    def kept(v):
        return pl.BlockSpec((BLOCK, own, chan), lambda i, s: (i + v[1], s[1], 0))

    def got(v):
        return pl.BlockSpec((BLOCK, own, chan), lambda i, s: (i + v[1], 0, 0))

    prod_spec = pl.BlockSpec((chan, BLOCK, wide), lambda i, s: (0, i, 0))
    out_spec = pl.BlockSpec((BLOCK, own, chan), lambda i, s: (i, 0, 0))
    pad = small[-1].shape[0]
    return pl.pallas_call(
        update_kernel,
        grid_spec=pltpu.PrefetchScalarGridSpec(
            num_scalar_prefetch=1,
            grid=(half // BLOCK,),
            in_specs=[prod_spec, prod_spec, kept(low), kept(high), got(low_got), got(high_got)]
            + [full_block(*v.shape) for v in small],
            out_specs=[
                out_spec,
                out_spec,
                pl.BlockSpec((heads, BLOCK, wide), lambda i, s: (0, i, 0)),
            ],
            scratch_shapes=[
                pltpu.VMEM((chan * BLOCK, wide), F32),
                pltpu.VMEM((pad * BLOCK, wide), F32),
                pltpu.VMEM((chan, BLOCK * wide), BF16),
                pltpu.VMEM((chan, BLOCK * wide), BF16),
                pltpu.VMEM((chan, BLOCK * wide), F32),
            ],
        ),
        out_shape=[
            jax.ShapeDtypeStruct((half, own, chan), BF16),
            jax.ShapeDtypeStruct((half, own, chan), BF16),
            jax.ShapeDtypeStruct((heads, half, wide), BF16),
        ],
        compiler_params=pltpu.CompilerParams(vmem_limit_bytes=VMEM),
        cost_estimate=pl.CostEstimate(
            flops=2 * half * wide * chan * chan * 3,
            bytes_accessed=2 * half * wide * chan * 5,
            transcendentals=half * wide * chan * 2,
        ),
    )(scalars, prod, prod_got, low[0], high[0], low_got[0], high_got[0], *small)


def table_kernel(sizes, scalars, *refs):
    groups, table = [refs[4 * i : 4 * i + 4] for i in range(len(sizes))], refs[-1]
    heads, count = table.shape[0], table.shape[1]
    wide = count // 2
    own = wide // 2
    length = scalars[0]
    for pair in range(2):
        first = pair * wide
        for group, members in zip(groups, sizes):
            start = 0
            for size in members:
                half = size // 2
                for side in range(2):
                    base = (first + side * half) % count
                    spot = lax.broadcasted_iota(jnp.int32, (half, wide), 0)
                    spot = spot + (scalars[3 + base // own] * own + base % own)
                    masked = jnp.where(spot < length, 0.0, -1e9 * LOG2E)
                    for h in range(heads):
                        parts = []
                        for j in range(2):
                            source = scalars[20 + 2 * pair + j]
                            value = group[0][h, start : start + half, :].astype(F32)
                            for d in range(1, 4):
                                other = group[d][h, start : start + half, :].astype(F32)
                                value = jnp.where(source == d, other, value)
                            parts.append(value[:, side * own : (side + 1) * own])
                        table[h, base : base + half, pair * wide : (pair + 1) * wide] = (
                            jnp.concatenate(parts, axis=1) * LOG2E + masked
                        )
                start += half
                first += size
    return


def bias_table(groups, sizes, scalars, heads, count):
    refs = [v for group in groups for v in group]
    return pl.pallas_call(
        functools.partial(table_kernel, sizes),
        grid_spec=pltpu.PrefetchScalarGridSpec(
            num_scalar_prefetch=1,
            grid=(1,),
            in_specs=[full_block(*v.shape) for v in refs],
            out_specs=full_block(heads, count, count),
        ),
        out_shape=jax.ShapeDtypeStruct((heads, count, count), F32),
        compiler_params=pltpu.CompilerParams(vmem_limit_bytes=VMEM),
        cost_estimate=pl.CostEstimate(
            flops=heads * count * count * 8,
            bytes_accessed=heads * count * count * 6,
            transcendentals=0,
        ),
    )(scalars, *refs)


def attention_kernel(parts, scalars, table, gain_ref, w_ref, wo_ref, *refs):
    pieces, outs = refs[:parts], refs[parts : parts + 4]
    work, result, keys, queries, values, gates, attended, scores_a, scores_b = refs[parts + 4 :]
    heads, count = table.shape[0], table.shape[1]
    chan = work.shape[1]
    own = outs[0].shape[0]
    depth = chan // heads
    first = 0
    for ref in pieces:
        size = ref.shape[0] * BLOCK
        work[first : first + size, :] = ref[...].astype(F32).reshape(size, chan)
        first += size

    def project(b, carry):
        normed = norm_columns(work[pl.ds(b, count, stride=BLOCK), :].T, gain_ref[...])
        every = jnp.dot(w_ref[...], normed, preferred_element_type=F32)
        queries[b] = (every[:chan] * (depth ** (-0.5) * LOG2E)).astype(BF16)
        keys[b] = every[chan : 2 * chan].astype(BF16).T
        values[b] = every[2 * chan : 3 * chan].astype(BF16)
        gates[b] = 0.5 * jnp.tanh(every[3 * chan :]) + 0.5
        return carry

    lax.fori_loop(0, BLOCK, project, 0, unroll=8)

    def score(b, out):
        for h in range(heads):
            alone = [queries[b, h * depth : (h + 1) * depth]]
            if h > 0:
                alone.insert(0, jnp.zeros((h * depth, count), BF16))
            if h < heads - 1:
                alone.append(jnp.zeros(((heads - 1 - h) * depth, count), BF16))
            alone = jnp.concatenate(alone, axis=0)
            out[h] = jnp.dot(keys[b], alone, preferred_element_type=F32) + table[h]

    def attend(b, scores):
        for h in range(heads):
            weights = jnp.exp2(scores[h] - jnp.max(scores[h], axis=0, keepdims=True))
            total = jnp.sum(weights, axis=0, keepdims=True)
            part = pl.ds(h * depth, depth)
            mixed = jnp.dot(values[b, part], weights.astype(BF16), preferred_element_type=F32)
            attended[b, part] = (mixed * (1.0 / total) * gates[b, part]).astype(BF16)

    score(0, scores_a)

    def two_columns(i, carry):
        b = 2 * i
        score(b + 1, scores_b)
        attend(b, scores_a)
        score(jnp.minimum(b + 2, BLOCK - 1), scores_a)
        attend(b + 1, scores_b)
        return carry

    lax.fori_loop(0, BLOCK // 2, two_columns, 0)

    def finish(b, carry):
        rows = pl.ds(b, count, stride=BLOCK)
        change = jnp.dot(wo_ref[...], attended[b], preferred_element_type=F32)
        result[rows, :] = work[rows, :] + change.T
        return carry

    lax.fori_loop(0, BLOCK, finish, 0, unroll=8)
    for d in range(4):
        rows = pl.ds(pl.multiple_of(scalars[7 + d] * (own * BLOCK), own * BLOCK), own * BLOCK)
        outs[d][...] = result[rows, :].reshape(own, BLOCK, chan).astype(BF16)


def attention(index, scalars, table, gain, w, wo, pieces):
    heads, count = table.shape[0], table.shape[1]
    own, chan = pieces[0].shape[1], pieces[0].shape[2]
    return pl.pallas_call(
        functools.partial(attention_kernel, len(pieces)),
        grid_spec=pltpu.PrefetchScalarGridSpec(
            num_scalar_prefetch=1,
            grid=(1,),
            in_specs=[full_block(*v.shape) for v in (table, gain, w, wo)]
            + [pl.BlockSpec((m.shape[0], BLOCK, chan), lambda i, s: (0, index, 0)) for m in pieces],
            out_specs=[full_block(own, BLOCK, chan)] * 4,
            scratch_shapes=[
                pltpu.VMEM((count * BLOCK, chan), F32),
                pltpu.VMEM((count * BLOCK, chan), F32),
                pltpu.VMEM((BLOCK, count, chan), BF16),
                pltpu.VMEM((BLOCK, chan, count), BF16),
                pltpu.VMEM((BLOCK, chan, count), BF16),
                pltpu.VMEM((BLOCK, chan, count), F32),
                pltpu.VMEM((BLOCK, chan, count), BF16),
                pltpu.VMEM((heads, count, count), F32),
                pltpu.VMEM((heads, count, count), F32),
            ],
        ),
        out_shape=[jax.ShapeDtypeStruct((own, BLOCK, chan), BF16)] * 4,
        compiler_params=pltpu.CompilerParams(vmem_limit_bytes=VMEM),
        cost_estimate=pl.CostEstimate(
            flops=2 * BLOCK * (count * chan * chan * 7 + 2 * heads * count * count * chan),
            bytes_accessed=2 * count * BLOCK * chan * 3,
            transcendentals=BLOCK * heads * count * count,
        ),
    )(scalars, table, gain, w, wo, *pieces)


def line_body(
    pair, lengths, gain_in, tri_in, tri_gate, gain_mid, tri_out, gain_att, att_in, att_bias, att_out
):
    own_rows = pair[0]
    own, count, chan = own_rows.shape
    heads = att_bias.shape[1]
    half = own // 2
    z = lax.axis_index("wide")
    inner = jnp.where(z < 2, 1, 2)
    partner = inner ^ 1
    other_in = 3 - inner
    other_out = other_in ^ 1
    order = jnp.stack([inner, partner, other_in, other_out])
    outer = ((z == 0) | (z == 3)).astype(jnp.int32)
    place = jnp.stack([jnp.argmax(order == (z + d) % 4) for d in range(4)])
    firsts = order * own
    scalars = jnp.concatenate(
        [
            lengths[:1],
            jnp.stack([inner, partner]),
            order,
            place,
            jnp.stack([outer]),
            firsts,
            firsts + half,
            (z - order) % 4,
        ]
    ).astype(jnp.int32)

    to_inner = [(0, 1), (3, 2)]
    to_outer = [(1, 0), (2, 3)]
    middle_link = [(1, 2), (2, 1)]

    def send(v, pairs):
        return lax.ppermute(v, "wide", pairs)

    def columns_of(v, device):
        return lax.dynamic_slice_in_dim(v, device * own, own, axis=1)

    def column(v):
        return v.reshape(chan, 1)

    own_halves = [own_rows[:half], own_rows[half:]]
    p_halves = [send(v, to_inner) for v in own_halves]
    oi_halves = [send(v, middle_link) for v in own_halves]
    oo_halves = [send(v, middle_link) for v in p_halves]

    own_got = send(columns_of(own_rows, partner), to_outer)
    p_got = columns_of(own_rows, z)
    oi_got = [send(columns_of(v, partner), to_outer) for v in oi_halves]
    oo_got = [send(columns_of(v, partner), to_outer) for v in oo_halves]

    tri_w = (jnp.swapaxes(tri_in, 1, 2).astype(F32) * 0.5).astype(BF16).reshape(4 * chan, chan)
    gain = column(gain_in)
    left_own, right_own = operands(own_rows, scalars, 12, gain, tri_w, 2)
    left_pa, right_pa = operands(p_halves[0], scalars, 13, gain, tri_w, 2)
    left_pb, right_pb = operands(p_halves[1], scalars, 17, gain, tri_w, 2)
    left_oi = [operands(v, scalars, k, gain, tri_w, 1)[0] for v, k in zip(oi_halves, (14, 18))]
    left_oo = [operands(v, scalars, k, gain, tri_w, 1)[0] for v, k in zip(oo_halves, (15, 19))]
    rights = [right_own, right_pa, right_pb]

    bias_w = jnp.zeros((8, chan), BF16).at[:heads].set(att_bias.T)
    small = [
        gain,
        column(gain_mid),
        column(gain_att),
        (tri_out.astype(F32) * 0.5).astype(BF16).T,
        (tri_gate.astype(F32) * 0.5).astype(BF16).T,
        bias_w,
    ]
    near, far = half // BLOCK, half // (2 * BLOCK)
    chunks = [
        ([left_own], (own_rows, 0), (own_rows, near), (own_got, 0), (own_got, near)),
        ([left_pa, left_pb], (p_halves[0], 0), (p_halves[1], 0), (p_got, 0), (p_got, near)),
        (left_oi, (oi_halves[0], 0), (oi_halves[1], 0), (oi_got[0], 0), (oi_got[1], 0)),
    ]
    for k in range(2):
        chunks.append(
            (
                [left_oo[k]],
                (oo_halves[k], 0),
                (oo_halves[k], far),
                (oo_got[k], 0),
                (oo_got[k], far),
            )
        )
    pieces, biases = [], []
    for lefts, low, high, low_got, high_got in chunks:
        kept, sent = products(lefts, rights)
        got = send(sent, to_outer)
        low, high, bias = updates(kept, got, low, high, low_got, high_got, scalars, small, heads)
        pieces += [low, high]
        biases.append(bias)

    groups, sizes = [], []
    for members in (biases[:3], biases[3:]):
        joined = jnp.concatenate(members, axis=1)
        others = [send(joined, [(i, (i + d) % 4) for i in range(4)]) for d in range(1, 4)]
        groups.append([joined] + others)
        sizes.append([2 * v.shape[1] for v in members])
    table = bias_table(groups, sizes, scalars, heads, count)

    att_w = jnp.swapaxes(att_in, 1, 2).astype(F32) * jnp.array([1, 1, 1, 0.5], F32).reshape(4, 1, 1)
    att_w = att_w.astype(BF16).reshape(4 * chan, chan)
    output = jnp.zeros((own, count, chan), BF16)
    for index in range(own // BLOCK):
        outs = attention(index, scalars, table, column(gain_att), att_w, att_out.T, pieces)
        for d in range(4):
            piece = outs[d]
            if d > 0:
                piece = send(piece, [(i, (i + d) % 4) for i in range(4)])
            source = (z - d) % 4
            output = lax.dynamic_update_slice(output, piece, (0, source * own + index * BLOCK, 0))
    return output[None]


def solution(mesh):
    in_specs = (
        P(("groups", "dp"), "wide", None, None),
        P(("groups", "dp")),
        P(),
        P(),
        P(),
        P(),
        P(),
        P(),
        P(),
        P(),
        P(),
    )
    out_specs = P(("groups", "dp"), "wide", None, None)
    body = line_body if mesh.shape["wide"] == 4 else general_body
    return jax.shard_map(body, mesh=mesh, in_specs=in_specs, out_specs=out_specs, check_vma=False)
```

```python
import functools
import math

import jax
import jax.numpy as jnp
from jax import lax
from jax.experimental import pallas as pl
from jax.experimental.pallas import tpu as pltpu
from jax.sharding import PartitionSpec as P

EPS = 1e-05
BLOCK = 16
LANES = 128
LOG2E = math.log2(math.e)
VMEM = 60 * 1024 * 1024
COST = pl.CostEstimate(flops=1024, bytes_accessed=1024, transcendentals=0)
F32 = jnp.float32
BF16 = jnp.bfloat16
NT = (((1,), (1,)), ((), ()))


def layer_norm(values, gain, axis):
    values = values.astype(jnp.float32)
    center = values - jnp.mean(values, axis=axis, keepdims=True)
    spread = jnp.mean(center * center, axis=axis, keepdims=True)
    shape = [1] * values.ndim
    shape[axis] = gain.shape[0]
    return center * lax.rsqrt(spread + EPS) * gain.reshape(shape)


def edge_operand(normed, weights, gate_index, proj_index, pair_mask):
    gate = jnp.einsum(
        "ikd,de->eik", normed, weights[gate_index], preferred_element_type=jnp.float32
    )
    proj = jnp.einsum(
        "ikd,de->eik", normed, weights[proj_index], preferred_element_type=jnp.float32
    )
    return (jax.nn.sigmoid(gate) * proj * pair_mask[None]).astype(jnp.bfloat16)


def row_update(block, normed, product, gain_mid, tri_out, tri_gate, gain_att, att_bias):
    mixed_in = layer_norm(product, gain_mid, 0).astype(jnp.bfloat16)
    update = jnp.einsum("cij,cd->ijd", mixed_in, tri_out, preferred_element_type=jnp.float32)
    gate = jax.nn.sigmoid(
        jnp.einsum("ijd,de->ije", normed, tri_gate, preferred_element_type=jnp.float32)
    )
    middle_rows = (block.astype(jnp.float32) + gate * update).astype(jnp.bfloat16)
    normed_rows = layer_norm(middle_rows, gain_att, 2).astype(jnp.bfloat16)
    bias_part = jnp.einsum(
        "ijc,ch->hij", normed_rows, att_bias, preferred_element_type=jnp.float32
    ).astype(jnp.bfloat16)
    return (middle_rows, bias_part)


def column_attention(normed, att_in, key_bias, heads):
    queries = jnp.einsum(
        "ijc,ce->jie", normed, att_in[0], preferred_element_type=jnp.float32
    ).astype(jnp.bfloat16)
    keys = jnp.einsum("ijc,ce->jie", normed, att_in[1], preferred_element_type=jnp.float32).astype(
        jnp.bfloat16
    )
    values = jnp.einsum(
        "ijc,ce->jie", normed, att_in[2], preferred_element_type=jnp.float32
    ).astype(jnp.bfloat16)
    gates = jax.nn.sigmoid(
        jnp.einsum("ijc,ce->jie", normed, att_in[3], preferred_element_type=jnp.float32)
    )
    count = queries.shape[1]
    width_all = queries.shape[2]
    depth = width_all // heads
    scale = depth ** (-0.5)

    def one_column(column):
        query, key, value, gate_col = column
        query = query.reshape(count, heads, depth)
        key = key.reshape(count, heads, depth)
        value = value.reshape(count, heads, depth)
        scores = (
            jnp.einsum("ihd,khd->hik", query, key, preferred_element_type=jnp.float32) * scale
            + key_bias
        )
        weights = jax.nn.softmax(scores, axis=-1).astype(jnp.bfloat16)
        mixed = jnp.einsum(
            "hik,khd->ihd", weights, value, preferred_element_type=jnp.float32
        ).reshape(count, width_all)
        return (gate_col * mixed).astype(jnp.bfloat16)

    return lax.map(one_column, (queries, keys, values, gates))


def general_body(
    pair, lengths, gain_in, tri_in, tri_gate, gain_mid, tri_out, gain_att, att_in, att_bias, att_out
):
    block = pair[0]
    rows = block.shape[0]
    count = block.shape[1]
    heads = att_bias.shape[1]
    first = lax.axis_index("wide") * rows
    mask = (jnp.arange(count) < lengths[0]).astype(jnp.float32)
    row_mask = lax.dynamic_slice_in_dim(mask, first, rows)
    pair_mask = row_mask[:, None] * mask[None, :]
    normed = layer_norm(block, gain_in, 2).astype(jnp.bfloat16)
    left = edge_operand(normed, tri_in, 0, 1, pair_mask)
    right = edge_operand(normed, tri_in, 2, 3, pair_mask)
    key_mask = ((mask - 1.0) * 1000000000.0)[None, None, :]
    left_ch, right_ch = (
        lax.all_to_all(left, "wide", split_axis=0, concat_axis=1, tiled=True),
        lax.all_to_all(right, "wide", split_axis=0, concat_axis=1, tiled=True),
    )
    product = jnp.einsum(
        "cik,cjk->cij", left_ch, right_ch, preferred_element_type=jnp.float32
    ).astype(jnp.bfloat16)
    product = lax.all_to_all(product, "wide", split_axis=1, concat_axis=0, tiled=True)
    middle_rows, bias_part = row_update(
        block, normed, product, gain_mid, tri_out, tri_gate, gain_att, att_bias
    )
    middle = lax.all_to_all(middle_rows, "wide", split_axis=1, concat_axis=0, tiled=True)
    table = lax.all_gather(bias_part, "wide", axis=1, tiled=True)
    normed_att = layer_norm(middle, gain_att, 2).astype(jnp.bfloat16)
    key_bias = jnp.swapaxes(table, 1, 2).astype(jnp.float32) + key_mask
    attended = column_attention(normed_att, att_in, key_bias, heads)
    result = jnp.einsum("jie,ec->ijc", attended, att_out, preferred_element_type=jnp.float32)
    finished = (middle.astype(jnp.float32) + result).astype(jnp.bfloat16)
    back = lax.all_to_all(finished, "wide", split_axis=0, concat_axis=1, tiled=True)
    return back[None]


def norm_columns(values, gain):
    center = values - jnp.mean(values, axis=0, keepdims=True)
    spread = jnp.mean(center * center, axis=0, keepdims=True)
    return (center * lax.rsqrt(spread + EPS) * gain).astype(BF16)


def full_block(*shape):
    return pl.BlockSpec(shape, lambda i, s: (0,) * len(shape))


def behind(kernel, position):
    def run(*refs):
        kernel(*refs[:position], *refs[position + 1 :])

    return run


ANYWHERE = pl.BlockSpec(memory_space=pl.ANY)


def nothing(*refs):
    return


def tie(x, after):
    return pl.pallas_call(
        nothing,
        in_specs=[ANYWHERE, ANYWHERE],
        out_specs=ANYWHERE,
        out_shape=jax.ShapeDtypeStruct(x.shape, x.dtype),
        input_output_aliases={0: 0},
    )(x, after)


def operand_kernel(sides, first_index, slices, scalars, x_ref, gain_ref, weight_ref, *refs):
    outs, cuts, works = refs[:sides], refs[sides : sides + len(slices)], refs[sides + len(slices) :]
    count, chan = x_ref.shape[1], x_ref.shape[2]
    length = scalars[0]
    row0 = scalars[first_index] + pl.program_id(0) * BLOCK
    key_mask = (lax.broadcasted_iota(jnp.int32, (1, count), 1) < length).astype(F32)
    for index, cut in zip(slices, cuts):
        own = cut.shape[1]
        cut[...] = x_ref[:, pl.ds(pl.multiple_of(scalars[index] * own, own), own), :]

    def step(r, carry):
        normed = norm_columns(x_ref[r].astype(F32).T, gain_ref[...])
        both = jnp.dot(weight_ref[...], normed, preferred_element_type=F32)
        row_mask = key_mask * (row0 + r < length).astype(F32)
        for side in range(sides):
            gate = both[2 * side * chan : (2 * side + 1) * chan]
            proj = both[(2 * side + 1) * chan : (2 * side + 2) * chan]
            value = (jnp.tanh(gate) + 1.0) * proj * row_mask
            for lane in range(count // LANES):
                works[side][lane, pl.ds(r, chan, stride=BLOCK), :] = value[
                    :, lane * LANES : (lane + 1) * LANES
                ]
        return carry

    lax.fori_loop(0, BLOCK, step, 0, unroll=8)
    for side in range(sides):
        for lane in range(count // LANES):
            outs[side][:, :, lane * LANES : (lane + 1) * LANES] = (
                works[side][lane].reshape(chan, BLOCK, LANES).astype(BF16)
            )


def operands(x, scalars, first_index, gain, weights, sides, slices, after):
    rows, count, chan = x.shape
    own = count // 4
    out = jax.ShapeDtypeStruct((chan, rows, count), BF16)
    cut = jax.ShapeDtypeStruct((rows, own, chan), BF16)
    return pl.pallas_call(
        behind(functools.partial(operand_kernel, sides, first_index, slices), 4),
        grid_spec=pltpu.PrefetchScalarGridSpec(
            num_scalar_prefetch=1,
            grid=(rows // BLOCK,),
            in_specs=[
                pl.BlockSpec((BLOCK, count, chan), lambda i, s: (i, 0, 0)),
                full_block(chan, 1),
                full_block(2 * sides * chan, chan),
                ANYWHERE,
            ],
            out_specs=[pl.BlockSpec((chan, BLOCK, count), lambda i, s: (0, i, 0))] * sides
            + [pl.BlockSpec((BLOCK, own, chan), lambda i, s: (i, 0, 0))] * len(slices),
            scratch_shapes=[pltpu.VMEM((count // LANES, chan * BLOCK, LANES), F32)] * sides,
        ),
        out_shape=[out] * sides + [cut] * len(slices),
        compiler_params=pltpu.CompilerParams(vmem_limit_bytes=VMEM),
        cost_estimate=COST,
    )(scalars, x, gain, weights[: 2 * sides * chan], after)


def product_kernel(members, rights, *refs):
    lefts = sum(members)
    left_refs, right_refs, outs = refs[:lefts], refs[lefts : lefts + rights], refs[lefts + rights :]
    own = right_refs[0].shape[1]
    for c in range(right_refs[0].shape[0]):
        left = [ref[c] for ref in left_refs]
        left = left[0] if lefts == 1 else jnp.concatenate(left, axis=0)
        right = jnp.concatenate([ref[c] for ref in right_refs], axis=0)
        prod = lax.dot_general(left, right, NT, preferred_element_type=F32)
        first = 0
        for g in range(len(members)):
            half = outs[2 * g].shape[1]
            low, high = prod[first : first + half], prod[first + half : first + 2 * half]
            first += 2 * half
            outs[2 * g][c] = jnp.concatenate([low[:, :own], high[:, :own]], axis=1).astype(BF16)
            outs[2 * g + 1][c] = jnp.concatenate([low[:, own:], high[:, own:]], axis=1).astype(BF16)


def products(groups, rights, after):
    lefts = [v for group in groups for v in group]
    chan, count = lefts[0].shape[0], lefts[0].shape[2]
    rows = [sum(v.shape[1] for v in group) for group in groups]
    own = rights[0].shape[1]
    step = 16
    spec = lambda v: pl.BlockSpec((step,) + v.shape[1:], lambda i: (i, 0, 0))
    outs = [jax.ShapeDtypeStruct((chan, r // 2, 2 * own), BF16) for r in rows for _ in range(2)]
    members = [len(group) for group in groups]
    return pl.pallas_call(
        behind(
            functools.partial(product_kernel, members, len(rights)), len(lefts) + len(rights)
        ),
        grid=(chan // step,),
        in_specs=[spec(v) for v in lefts + rights] + [ANYWHERE],
        out_specs=[spec(v) for v in outs],
        out_shape=outs,
        compiler_params=pltpu.CompilerParams(vmem_limit_bytes=VMEM),
        cost_estimate=COST,
    )(*lefts, *rights, after)


def update_kernel(
    scalars,
    prod_ref,
    prod_got_ref,
    low_ref,
    high_ref,
    low_got_ref,
    high_got_ref,
    gain_in_ref,
    gain_mid_ref,
    gain_att_ref,
    out_w_ref,
    gate_w_ref,
    bias_w_ref,
    low_out,
    high_out,
    bias_ref,
    work,
    bias_work,
    normed_work,
    mixed_work,
    x_work,
):
    chan, _, wide = prod_ref.shape
    heads = bias_ref.shape[0]
    pad = bias_w_ref.shape[0]
    own = wide // 2
    outer = scalars[7] != 0

    @pl.when(outer)
    def _():
        work[...] = prod_got_ref[...].astype(F32).reshape(chan * BLOCK, wide)

    @pl.when(jnp.logical_not(outer))
    def _():
        work[...] = prod_ref[...].astype(F32).reshape(chan * BLOCK, wide)

    def load(r, carry):
        lane = pl.ds(pl.multiple_of(r * wide, wide), wide)
        mixed_work[:, lane] = norm_columns(work[pl.ds(r, chan, stride=BLOCK), :], gain_mid_ref[...])
        low = jnp.where(outer, low_got_ref[r], low_ref[r])
        high = jnp.where(outer, high_got_ref[r], high_ref[r])
        x = jnp.concatenate([low, high], axis=0).astype(F32).T
        x_work[:, lane] = x
        normed_work[:, lane] = norm_columns(x, gain_in_ref[...])
        return carry

    lax.fori_loop(0, BLOCK, load, 0, unroll=4)
    group = 8

    def update(j, carry):
        lane = pl.ds(pl.multiple_of(j * group * wide, group * wide), group * wide)
        gate = jnp.tanh(jnp.dot(gate_w_ref[...], normed_work[:, lane], preferred_element_type=F32))
        change = jnp.dot(out_w_ref[...], mixed_work[:, lane], preferred_element_type=F32)
        middle = (x_work[:, lane] + (gate + 1.0) * change).astype(BF16).astype(F32)
        normed_att = norm_columns(middle, gain_att_ref[...])
        bias = jnp.dot(bias_w_ref[...], normed_att, preferred_element_type=F32)
        for i in range(group):
            r = j * group + i
            turned = middle[:, i * wide : (i + 1) * wide].T.astype(BF16)
            low_out[r] = turned[:own]
            high_out[r] = turned[own:]
            bias_work[pl.ds(r, pad, stride=BLOCK), :] = bias[:, i * wide : (i + 1) * wide]
        return carry

    lax.fori_loop(0, BLOCK // group, update, 0)
    bias_ref[...] = bias_work[: heads * BLOCK, :].reshape(heads, BLOCK, wide).astype(BF16)


def updates(prod, prod_got, low, high, low_got, high_got, scalars, small, heads, after):
    chan, half, wide = prod.shape
    own = wide // 2

    def kept(v):
        return pl.BlockSpec((BLOCK, own, chan), lambda i, s: (i + v[1], s[1], 0))

    def got(v):
        return pl.BlockSpec((BLOCK, own, chan), lambda i, s: (i + v[1], 0, 0))

    prod_spec = pl.BlockSpec((chan, BLOCK, wide), lambda i, s: (0, i, 0))
    out_spec = pl.BlockSpec((BLOCK, own, chan), lambda i, s: (i, 0, 0))
    pad = small[-1].shape[0]
    return pl.pallas_call(
        behind(update_kernel, 7 + len(small)),
        grid_spec=pltpu.PrefetchScalarGridSpec(
            num_scalar_prefetch=1,
            grid=(half // BLOCK,),
            in_specs=[prod_spec, prod_spec, kept(low), kept(high), got(low_got), got(high_got)]
            + [full_block(*v.shape) for v in small]
            + [ANYWHERE],
            out_specs=[
                out_spec,
                out_spec,
                pl.BlockSpec((heads, BLOCK, wide), lambda i, s: (0, i, 0)),
            ],
            scratch_shapes=[
                pltpu.VMEM((chan * BLOCK, wide), F32),
                pltpu.VMEM((pad * BLOCK, wide), F32),
                pltpu.VMEM((chan, BLOCK * wide), BF16),
                pltpu.VMEM((chan, BLOCK * wide), BF16),
                pltpu.VMEM((chan, BLOCK * wide), F32),
            ],
        ),
        out_shape=[
            jax.ShapeDtypeStruct((half, own, chan), BF16),
            jax.ShapeDtypeStruct((half, own, chan), BF16),
            jax.ShapeDtypeStruct((heads, half, wide), BF16),
        ],
        compiler_params=pltpu.CompilerParams(vmem_limit_bytes=VMEM),
        cost_estimate=COST,
    )(scalars, prod, prod_got, low[0], high[0], low_got[0], high_got[0], *small, after)


def table_kernel(sizes, scalars, *refs):
    groups, table = [refs[4 * i : 4 * i + 4] for i in range(len(sizes))], refs[-1]
    heads, count = table.shape[0], table.shape[1]
    wide = count // 2
    own = wide // 2
    length = scalars[0]
    for pair in range(2):
        first = pair * wide
        for group, members in zip(groups, sizes):
            start = 0
            for size in members:
                half = size // 2
                for side in range(2):
                    base = (first + side * half) % count
                    spot = lax.broadcasted_iota(jnp.int32, (half, wide), 0)
                    spot = spot + (scalars[3 + base // own] * own + base % own)
                    masked = jnp.where(spot < length, 0.0, -1e9 * LOG2E)
                    for h in range(heads):
                        parts = []
                        for j in range(2):
                            source = scalars[16 + 2 * pair + j]
                            value = group[0][h, start : start + half, :].astype(F32)
                            for d in range(1, 4):
                                other = group[d][h, start : start + half, :].astype(F32)
                                value = jnp.where(source == d, other, value)
                            parts.append(value[:, side * own : (side + 1) * own])
                        table[h, base : base + half, pair * wide : (pair + 1) * wide] = (
                            jnp.concatenate(parts, axis=1) * LOG2E + masked
                        )
                start += half
                first += size
    return


def bias_table(groups, sizes, scalars, heads, count):
    refs = [v for group in groups for v in group]
    return pl.pallas_call(
        functools.partial(table_kernel, sizes),
        grid_spec=pltpu.PrefetchScalarGridSpec(
            num_scalar_prefetch=1,
            grid=(1,),
            in_specs=[full_block(*v.shape) for v in refs],
            out_specs=full_block(heads, count, count),
        ),
        out_shape=jax.ShapeDtypeStruct((heads, count, count), F32),
        compiler_params=pltpu.CompilerParams(vmem_limit_bytes=VMEM),
        cost_estimate=COST,
    )(scalars, *refs)


def attention_kernel(parts, scalars, table, gain_ref, w_ref, wo_ref, *refs):
    pieces, outs = refs[:parts], refs[parts : parts + 4]
    work, result, keys, queries, values, gates, attended, scores_a, scores_b = refs[parts + 4 :]
    heads, count = table.shape[0], table.shape[1]
    chan = work.shape[1]
    own = count // 4
    depth = chan // heads
    first = 0
    for ref in pieces:
        size = ref.shape[0] * BLOCK
        work[first : first + size, :] = ref[...].astype(F32).reshape(size, chan)
        first += size

    def project(b, carry):
        normed = norm_columns(work[pl.ds(b, count, stride=BLOCK), :].T, gain_ref[...])
        every = jnp.dot(w_ref[...], normed, preferred_element_type=F32)
        queries[b] = (every[:chan] * (depth ** (-0.5) * LOG2E)).astype(BF16)
        keys[b] = every[chan : 2 * chan].astype(BF16).T
        values[b] = every[2 * chan : 3 * chan].astype(BF16)
        gates[b] = 0.5 * jnp.tanh(every[3 * chan :]) + 0.5
        return carry

    lax.fori_loop(0, BLOCK, project, 0, unroll=8)

    def score(b, out):
        for h in range(heads):
            alone = [queries[b, h * depth : (h + 1) * depth]]
            if h > 0:
                alone.insert(0, jnp.zeros((h * depth, count), BF16))
            if h < heads - 1:
                alone.append(jnp.zeros(((heads - 1 - h) * depth, count), BF16))
            alone = jnp.concatenate(alone, axis=0)
            out[h] = jnp.dot(keys[b], alone, preferred_element_type=F32) + table[h]

    def attend(b, scores):
        for h in range(heads):
            weights = jnp.exp2(scores[h] - jnp.max(scores[h], axis=0, keepdims=True))
            total = jnp.sum(weights, axis=0, keepdims=True)
            part = pl.ds(h * depth, depth)
            mixed = jnp.dot(values[b, part], weights.astype(BF16), preferred_element_type=F32)
            attended[b, part] = (mixed * (1.0 / total) * gates[b, part]).astype(BF16)

    score(0, scores_a)

    def two_columns(i, carry):
        b = 2 * i
        score(b + 1, scores_b)
        attend(b, scores_a)
        score(jnp.minimum(b + 2, BLOCK - 1), scores_a)
        attend(b + 1, scores_b)
        return carry

    lax.fori_loop(0, BLOCK // 2, two_columns, 0)

    def finish(b, carry):
        rows = pl.ds(b, count, stride=BLOCK)
        change = jnp.dot(wo_ref[...], attended[b], preferred_element_type=F32)
        result[rows, :] = work[rows, :] + change.T
        return carry

    lax.fori_loop(0, BLOCK, finish, 0, unroll=8)
    for d in range(4):
        rows = pl.ds(pl.multiple_of(scalars[21 + d] * (own * BLOCK), own * BLOCK), own * BLOCK)
        outs[d][...] = result[rows, :].reshape(own, BLOCK, chan).astype(BF16)


def attention(index, scalars, table, gain, w, wo, pieces):
    heads, count = table.shape[0], table.shape[1]
    own, chan = pieces[0].shape[1], pieces[0].shape[2]
    return pl.pallas_call(
        functools.partial(attention_kernel, len(pieces)),
        grid_spec=pltpu.PrefetchScalarGridSpec(
            num_scalar_prefetch=1,
            grid=(1,),
            in_specs=[full_block(*v.shape) for v in (table, gain, w, wo)]
            + [pl.BlockSpec((m.shape[0], BLOCK, chan), lambda i, s: (0, index, 0)) for m in pieces],
            out_specs=[full_block(own, BLOCK, chan)] * 4,
            scratch_shapes=[
                pltpu.VMEM((count * BLOCK, chan), F32),
                pltpu.VMEM((count * BLOCK, chan), F32),
                pltpu.VMEM((BLOCK, count, chan), BF16),
                pltpu.VMEM((BLOCK, chan, count), BF16),
                pltpu.VMEM((BLOCK, chan, count), BF16),
                pltpu.VMEM((BLOCK, chan, count), F32),
                pltpu.VMEM((BLOCK, chan, count), BF16),
                pltpu.VMEM((heads, count, count), F32),
                pltpu.VMEM((heads, count, count), F32),
            ],
        ),
        out_shape=[jax.ShapeDtypeStruct((own, BLOCK, chan), BF16)] * 4,
        compiler_params=pltpu.CompilerParams(vmem_limit_bytes=VMEM),
        cost_estimate=COST,
    )(scalars, table, gain, w, wo, *pieces)


def place_kernel(index, scalars, *refs):
    output, sems = refs[-2:]
    copies = []
    for d in range(4):
        own = refs[d].shape[0]
        first = pl.multiple_of(scalars[25 + d] * own + index * BLOCK, BLOCK)
        copies.append(
            pltpu.make_async_copy(refs[d], output.at[:, pl.ds(first, BLOCK), :], sems.at[d])
        )
    for copy in copies:
        copy.start()
    for copy in copies:
        copy.wait()


def place(got, output, index, scalars):
    own, _, chan = got[0].shape
    rest = [] if output is None else [output]
    return pl.pallas_call(
        functools.partial(place_kernel, index),
        grid_spec=pltpu.PrefetchScalarGridSpec(
            num_scalar_prefetch=1,
            grid=(1,),
            in_specs=[full_block(*v.shape) for v in got] + [ANYWHERE] * len(rest),
            out_specs=ANYWHERE,
            scratch_shapes=[pltpu.SemaphoreType.DMA((4,))],
        ),
        out_shape=jax.ShapeDtypeStruct((own, 4 * own, chan), BF16),
        input_output_aliases={5: 0} if rest else {},
        cost_estimate=COST,
    )(scalars, *got, *rest)


def line_body(
    pair, lengths, gain_in, tri_in, tri_gate, gain_mid, tri_out, gain_att, att_in, att_bias, att_out
):
    own_rows = pair[0]
    own, count, chan = own_rows.shape
    heads = att_bias.shape[1]
    half = own // 2
    z = lax.axis_index("wide")
    inner = jnp.where(z < 2, 1, 2)
    partner = inner ^ 1
    other_in = 3 - inner
    other_out = other_in ^ 1
    order = jnp.stack([inner, partner, other_in, other_out])
    outer = ((z == 0) | (z == 3)).astype(jnp.int32)
    firsts = order * own
    scalars = jnp.concatenate(
        [
            lengths[:1],
            jnp.stack([inner, partner]),
            order,
            jnp.stack([outer]),
            firsts,
            firsts + half,
            (z - order) % 4,
            jnp.stack([z]),
            jnp.stack([jnp.argmax(order == (z + d) % 4) for d in range(4)]),
            (z - jnp.arange(4)) % 4,
        ]
    ).astype(jnp.int32)

    to_inner = [(0, 1), (3, 2)]
    to_outer = [(1, 0), (2, 3)]
    middle_link = [(1, 2), (2, 1)]

    def send(v, pairs):
        return lax.ppermute(v, "wide", pairs)

    def column(v):
        return v.reshape(chan, 1)

    tri_w = (jnp.swapaxes(tri_in, 1, 2).astype(F32) * 0.5).astype(BF16).reshape(4 * chan, chan)
    gain = column(gain_in)

    oi_rows = send(own_rows, middle_link)
    p_halves = [send(v, to_inner) for v in (own_rows[:half], own_rows[half:])]
    left_own, right_own, own_cut, p_got = operands(
        own_rows, scalars, 8, gain, tri_w, 2, (2, 20), scalars
    )
    own_got = send(own_cut, to_outer)
    p_halves[0] = tie(p_halves[0], left_own)
    left_pa, right_pa = operands(p_halves[0], scalars, 9, gain, tri_w, 2, (), scalars)
    p_halves[1] = tie(p_halves[1], left_pa)
    oo_halves = [send(v, middle_link) for v in p_halves]

    bias_w = jnp.zeros((8, chan), BF16).at[:heads].set(att_bias.T)
    small = [
        gain,
        column(gain_mid),
        column(gain_att),
        (tri_out.astype(F32) * 0.5).astype(BF16).T,
        (tri_gate.astype(F32) * 0.5).astype(BF16).T,
        bias_w,
    ]
    near, far = half // BLOCK, half // (2 * BLOCK)
    pieces, biases = [], []

    left_pb, right_pb = operands(p_halves[1], scalars, 13, gain, tri_w, 2, (), left_pa)
    rights = [right_own, right_pa, right_pb]
    kept_own, sent_own, kept_p, sent_p = products([[left_own], [left_pa, left_pb]], rights, scalars)
    left_oi, oi_cut = operands(oi_rows, scalars, 10, gain, tri_w, 1, (2,), kept_p)
    oi_got = send(oi_cut, to_outer)
    left_a, a_cut = operands(oo_halves[0], scalars, 11, gain, tri_w, 1, (2,), left_oi)
    oo_got = [send(a_cut, to_outer)]
    kept_oi, sent_oi, kept_a, sent_a = products([[left_oi], [left_a]], rights, scalars)

    def update(kept, sent, low, high, low_got, high_got, after):
        got = send(sent, to_outer)
        low, high, bias = updates(
            kept, got, low, high, low_got, high_got, scalars, small, heads, after
        )
        pieces.extend([low, high])
        biases.append(bias)
        return bias

    last = update(
        kept_own, sent_own, (own_rows, 0), (own_rows, near), (own_got, 0), (own_got, near), kept_oi
    )
    last = update(
        kept_p, sent_p, (p_halves[0], 0), (p_halves[1], 0), (p_got, 0), (p_got, near), last
    )
    left_b, b_cut = operands(oo_halves[1], scalars, 15, gain, tri_w, 1, (2,), last)
    oo_got.append(send(b_cut, to_outer))
    kept_b, sent_b = products([[left_b]], rights, last)
    last = update(
        kept_oi, sent_oi, (oi_rows, 0), (oi_rows, near), (oi_got, 0), (oi_got, near), kept_b
    )
    for k, (kept, sent) in enumerate(((kept_a, sent_a), (kept_b, sent_b))):
        low, low_got = oo_halves[k], oo_got[k]
        last = update(kept, sent, (low, 0), (low, far), (low_got, 0), (low_got, far), last)

    groups, sizes = [], []
    for members in (biases[:4], biases[4:]):
        joined = jnp.concatenate(members, axis=1)
        others = [send(joined, [(i, (i + d) % 4) for i in range(4)]) for d in range(1, 4)]
        groups.append([joined] + others)
        sizes.append([2 * v.shape[1] for v in members])
    table = bias_table(groups, sizes, scalars, heads, count)

    att_w = jnp.swapaxes(att_in, 1, 2).astype(F32) * jnp.array([1, 1, 1, 0.5], F32).reshape(4, 1, 1)
    att_w = att_w.astype(BF16).reshape(4 * chan, chan)
    output = None
    for index in range(own // BLOCK):
        got = list(attention(index, scalars, table, column(gain_att), att_w, att_out.T, pieces))
        for d in range(1, 4):
            got[d] = send(got[d], [(i, (i + d) % 4) for i in range(4)])
        output = place(got, output, index, scalars)
    return output[None]


def solution(mesh):
    in_specs = (
        P(("groups", "dp"), "wide", None, None),
        P(("groups", "dp")),
        P(),
        P(),
        P(),
        P(),
        P(),
        P(),
        P(),
        P(),
        P(),
    )
    out_specs = P(("groups", "dp"), "wide", None, None)
    body = line_body if mesh.shape["wide"] == 4 else general_body
    return jax.shard_map(body, mesh=mesh, in_specs=in_specs, out_specs=out_specs, check_vma=False)
```

```python
import functools
import math

import jax
import jax.numpy as jnp
from jax import lax
from jax.experimental import pallas as pl
from jax.experimental.pallas import tpu as pltpu
from jax.sharding import PartitionSpec as P

EPS = 1e-05
BLOCK = 16
LANES = 128
LOG2E = math.log2(math.e)
VMEM = 60 * 1024 * 1024
COST = pl.CostEstimate(flops=1024, bytes_accessed=1024, transcendentals=0)
F32 = jnp.float32
BF16 = jnp.bfloat16
NT = (((1,), (1,)), ((), ()))


def layer_norm(values, gain, axis):
    values = values.astype(jnp.float32)
    center = values - jnp.mean(values, axis=axis, keepdims=True)
    spread = jnp.mean(center * center, axis=axis, keepdims=True)
    shape = [1] * values.ndim
    shape[axis] = gain.shape[0]
    return center * lax.rsqrt(spread + EPS) * gain.reshape(shape)


def edge_operand(normed, weights, gate_index, proj_index, pair_mask):
    gate = jnp.einsum(
        "ikd,de->eik", normed, weights[gate_index], preferred_element_type=jnp.float32
    )
    proj = jnp.einsum(
        "ikd,de->eik", normed, weights[proj_index], preferred_element_type=jnp.float32
    )
    return (jax.nn.sigmoid(gate) * proj * pair_mask[None]).astype(jnp.bfloat16)


def row_update(block, normed, product, gain_mid, tri_out, tri_gate, gain_att, att_bias):
    mixed_in = layer_norm(product, gain_mid, 0).astype(jnp.bfloat16)
    update = jnp.einsum("cij,cd->ijd", mixed_in, tri_out, preferred_element_type=jnp.float32)
    gate = jax.nn.sigmoid(
        jnp.einsum("ijd,de->ije", normed, tri_gate, preferred_element_type=jnp.float32)
    )
    middle_rows = (block.astype(jnp.float32) + gate * update).astype(jnp.bfloat16)
    normed_rows = layer_norm(middle_rows, gain_att, 2).astype(jnp.bfloat16)
    bias_part = jnp.einsum(
        "ijc,ch->hij", normed_rows, att_bias, preferred_element_type=jnp.float32
    ).astype(jnp.bfloat16)
    return (middle_rows, bias_part)


def column_attention(normed, att_in, key_bias, heads):
    queries = jnp.einsum(
        "ijc,ce->jie", normed, att_in[0], preferred_element_type=jnp.float32
    ).astype(jnp.bfloat16)
    keys = jnp.einsum("ijc,ce->jie", normed, att_in[1], preferred_element_type=jnp.float32).astype(
        jnp.bfloat16
    )
    values = jnp.einsum(
        "ijc,ce->jie", normed, att_in[2], preferred_element_type=jnp.float32
    ).astype(jnp.bfloat16)
    gates = jax.nn.sigmoid(
        jnp.einsum("ijc,ce->jie", normed, att_in[3], preferred_element_type=jnp.float32)
    )
    count = queries.shape[1]
    width_all = queries.shape[2]
    depth = width_all // heads
    scale = depth ** (-0.5)

    def one_column(column):
        query, key, value, gate_col = column
        query = query.reshape(count, heads, depth)
        key = key.reshape(count, heads, depth)
        value = value.reshape(count, heads, depth)
        scores = (
            jnp.einsum("ihd,khd->hik", query, key, preferred_element_type=jnp.float32) * scale
            + key_bias
        )
        weights = jax.nn.softmax(scores, axis=-1).astype(jnp.bfloat16)
        mixed = jnp.einsum(
            "hik,khd->ihd", weights, value, preferred_element_type=jnp.float32
        ).reshape(count, width_all)
        return (gate_col * mixed).astype(jnp.bfloat16)

    return lax.map(one_column, (queries, keys, values, gates))


def general_body(
    pair, lengths, gain_in, tri_in, tri_gate, gain_mid, tri_out, gain_att, att_in, att_bias, att_out
):
    block = pair[0]
    rows = block.shape[0]
    count = block.shape[1]
    heads = att_bias.shape[1]
    first = lax.axis_index("wide") * rows
    mask = (jnp.arange(count) < lengths[0]).astype(jnp.float32)
    row_mask = lax.dynamic_slice_in_dim(mask, first, rows)
    pair_mask = row_mask[:, None] * mask[None, :]
    normed = layer_norm(block, gain_in, 2).astype(jnp.bfloat16)
    left = edge_operand(normed, tri_in, 0, 1, pair_mask)
    right = edge_operand(normed, tri_in, 2, 3, pair_mask)
    key_mask = ((mask - 1.0) * 1000000000.0)[None, None, :]
    left_ch, right_ch = (
        lax.all_to_all(left, "wide", split_axis=0, concat_axis=1, tiled=True),
        lax.all_to_all(right, "wide", split_axis=0, concat_axis=1, tiled=True),
    )
    product = jnp.einsum(
        "cik,cjk->cij", left_ch, right_ch, preferred_element_type=jnp.float32
    ).astype(jnp.bfloat16)
    product = lax.all_to_all(product, "wide", split_axis=1, concat_axis=0, tiled=True)
    middle_rows, bias_part = row_update(
        block, normed, product, gain_mid, tri_out, tri_gate, gain_att, att_bias
    )
    middle = lax.all_to_all(middle_rows, "wide", split_axis=1, concat_axis=0, tiled=True)
    table = lax.all_gather(bias_part, "wide", axis=1, tiled=True)
    normed_att = layer_norm(middle, gain_att, 2).astype(jnp.bfloat16)
    key_bias = jnp.swapaxes(table, 1, 2).astype(jnp.float32) + key_mask
    attended = column_attention(normed_att, att_in, key_bias, heads)
    result = jnp.einsum("jie,ec->ijc", attended, att_out, preferred_element_type=jnp.float32)
    finished = (middle.astype(jnp.float32) + result).astype(jnp.bfloat16)
    back = lax.all_to_all(finished, "wide", split_axis=0, concat_axis=1, tiled=True)
    return back[None]


def norm_columns(values, gain):
    center = values - jnp.mean(values, axis=0, keepdims=True)
    spread = jnp.mean(center * center, axis=0, keepdims=True)
    return (center * lax.rsqrt(spread + EPS) * gain).astype(BF16)


def full_block(*shape):
    return pl.BlockSpec(shape, lambda i, s: (0,) * len(shape))


def behind(kernel, position, after):
    def run(*refs):
        kernel(*refs[:position], *refs[position + len(after) :])

    return run


ANYWHERE = pl.BlockSpec(memory_space=pl.ANY)


def nothing(*refs):
    return


def tie(x, *after):
    return pl.pallas_call(
        nothing,
        in_specs=[ANYWHERE] * (1 + len(after)),
        out_specs=ANYWHERE,
        out_shape=jax.ShapeDtypeStruct(x.shape, x.dtype),
        input_output_aliases={0: 0},
    )(x, *after)


def operand_kernel(sides, first_index, slices, scalars, x_ref, gain_ref, weight_ref, *refs):
    outs, cuts, works = refs[:sides], refs[sides : sides + len(slices)], refs[sides + len(slices) :]
    count, chan = x_ref.shape[1], x_ref.shape[2]
    length = scalars[0]
    row0 = scalars[first_index] + pl.program_id(0) * BLOCK
    key_mask = (lax.broadcasted_iota(jnp.int32, (1, count), 1) < length).astype(F32)
    for index, cut in zip(slices, cuts):
        own = cut.shape[1]
        cut[...] = x_ref[:, pl.ds(pl.multiple_of(scalars[index] * own, own), own), :]

    def step(r, carry):
        normed = norm_columns(x_ref[r].astype(F32).T, gain_ref[...])
        both = jnp.dot(weight_ref[...], normed, preferred_element_type=F32)
        row_mask = key_mask * (row0 + r < length).astype(F32)
        for side in range(sides):
            gate = both[2 * side * chan : (2 * side + 1) * chan]
            proj = both[(2 * side + 1) * chan : (2 * side + 2) * chan]
            value = (jnp.tanh(gate) + 1.0) * proj * row_mask
            for lane in range(count // LANES):
                works[side][lane, pl.ds(r, chan, stride=BLOCK), :] = value[
                    :, lane * LANES : (lane + 1) * LANES
                ]
        return carry

    lax.fori_loop(0, BLOCK, step, 0, unroll=8)
    for side in range(sides):
        for lane in range(count // LANES):
            outs[side][:, :, lane * LANES : (lane + 1) * LANES] = (
                works[side][lane].reshape(chan, BLOCK, LANES).astype(BF16)
            )


def operands(x, scalars, first_index, gain, weights, sides, slices, *after):
    rows, count, chan = x.shape
    own = count // 4
    out = jax.ShapeDtypeStruct((chan, rows, count), BF16)
    cut = jax.ShapeDtypeStruct((rows, own, chan), BF16)
    return pl.pallas_call(
        behind(functools.partial(operand_kernel, sides, first_index, slices), 4, after),
        grid_spec=pltpu.PrefetchScalarGridSpec(
            num_scalar_prefetch=1,
            grid=(rows // BLOCK,),
            in_specs=[
                pl.BlockSpec((BLOCK, count, chan), lambda i, s: (i, 0, 0)),
                full_block(chan, 1),
                full_block(2 * sides * chan, chan),
            ]
            + [ANYWHERE] * len(after),
            out_specs=[pl.BlockSpec((chan, BLOCK, count), lambda i, s: (0, i, 0))] * sides
            + [pl.BlockSpec((BLOCK, own, chan), lambda i, s: (i, 0, 0))] * len(slices),
            scratch_shapes=[pltpu.VMEM((count // LANES, chan * BLOCK, LANES), F32)] * sides,
        ),
        out_shape=[out] * sides + [cut] * len(slices),
        compiler_params=pltpu.CompilerParams(vmem_limit_bytes=VMEM),
        cost_estimate=COST,
    )(scalars, x, gain, weights[: 2 * sides * chan], *after)


def product_kernel(members, rights, *refs):
    lefts = sum(members)
    left_refs, right_refs, outs = refs[:lefts], refs[lefts : lefts + rights], refs[lefts + rights :]
    own = right_refs[0].shape[1]
    for c in range(right_refs[0].shape[0]):
        left = [ref[c] for ref in left_refs]
        left = left[0] if lefts == 1 else jnp.concatenate(left, axis=0)
        right = jnp.concatenate([ref[c] for ref in right_refs], axis=0)
        prod = lax.dot_general(left, right, NT, preferred_element_type=F32)
        first = 0
        for g in range(len(members)):
            half = outs[2 * g].shape[1]
            low, high = prod[first : first + half], prod[first + half : first + 2 * half]
            first += 2 * half
            outs[2 * g][c] = jnp.concatenate([low[:, :own], high[:, :own]], axis=1).astype(BF16)
            outs[2 * g + 1][c] = jnp.concatenate([low[:, own:], high[:, own:]], axis=1).astype(BF16)


def products(groups, rights, *after):
    lefts = [v for group in groups for v in group]
    chan, count = lefts[0].shape[0], lefts[0].shape[2]
    rows = [sum(v.shape[1] for v in group) for group in groups]
    own = rights[0].shape[1]
    step = 16
    spec = lambda v: pl.BlockSpec((step,) + v.shape[1:], lambda i: (i, 0, 0))
    outs = [jax.ShapeDtypeStruct((chan, r // 2, 2 * own), BF16) for r in rows for _ in range(2)]
    members = [len(group) for group in groups]
    return pl.pallas_call(
        behind(
            functools.partial(product_kernel, members, len(rights)),
            len(lefts) + len(rights),
            after,
        ),
        grid=(chan // step,),
        in_specs=[spec(v) for v in lefts + rights] + [ANYWHERE] * len(after),
        out_specs=[spec(v) for v in outs],
        out_shape=outs,
        compiler_params=pltpu.CompilerParams(vmem_limit_bytes=VMEM),
        cost_estimate=COST,
    )(*lefts, *rights, *after)


def update_kernel(
    scalars,
    prod_ref,
    prod_got_ref,
    low_ref,
    high_ref,
    low_got_ref,
    high_got_ref,
    gain_in_ref,
    gain_mid_ref,
    gain_att_ref,
    out_w_ref,
    gate_w_ref,
    bias_w_ref,
    low_out,
    high_out,
    bias_ref,
    work,
    bias_work,
    normed_work,
    mixed_work,
    x_work,
):
    chan, _, wide = prod_ref.shape
    heads = bias_ref.shape[0]
    pad = bias_w_ref.shape[0]
    own = wide // 2
    outer = scalars[7] != 0

    @pl.when(outer)
    def _():
        work[...] = prod_got_ref[...].astype(F32).reshape(chan * BLOCK, wide)

    @pl.when(jnp.logical_not(outer))
    def _():
        work[...] = prod_ref[...].astype(F32).reshape(chan * BLOCK, wide)

    def load(r, carry):
        lane = pl.ds(pl.multiple_of(r * wide, wide), wide)
        mixed_work[:, lane] = norm_columns(work[pl.ds(r, chan, stride=BLOCK), :], gain_mid_ref[...])
        low = jnp.where(outer, low_got_ref[r], low_ref[r])
        high = jnp.where(outer, high_got_ref[r], high_ref[r])
        x = jnp.concatenate([low, high], axis=0).astype(F32).T
        x_work[:, lane] = x
        normed_work[:, lane] = norm_columns(x, gain_in_ref[...])
        return carry

    lax.fori_loop(0, BLOCK, load, 0, unroll=4)
    group = 8

    def update(j, carry):
        lane = pl.ds(pl.multiple_of(j * group * wide, group * wide), group * wide)
        gate = jnp.tanh(jnp.dot(gate_w_ref[...], normed_work[:, lane], preferred_element_type=F32))
        change = jnp.dot(out_w_ref[...], mixed_work[:, lane], preferred_element_type=F32)
        middle = (x_work[:, lane] + (gate + 1.0) * change).astype(BF16).astype(F32)
        normed_att = norm_columns(middle, gain_att_ref[...])
        bias = jnp.dot(bias_w_ref[...], normed_att, preferred_element_type=F32)
        for i in range(group):
            r = j * group + i
            turned = middle[:, i * wide : (i + 1) * wide].T.astype(BF16)
            low_out[r] = turned[:own]
            high_out[r] = turned[own:]
            bias_work[pl.ds(r, pad, stride=BLOCK), :] = bias[:, i * wide : (i + 1) * wide]
        return carry

    lax.fori_loop(0, BLOCK // group, update, 0)
    bias_ref[...] = bias_work[: heads * BLOCK, :].reshape(heads, BLOCK, wide).astype(BF16)


def updates(prod, prod_got, low, high, low_got, high_got, scalars, small, heads, *after):
    chan, half, wide = prod.shape
    own = wide // 2

    def kept(v):
        return pl.BlockSpec((BLOCK, own, chan), lambda i, s: (i + v[1], s[1], 0))

    def got(v):
        return pl.BlockSpec((BLOCK, own, chan), lambda i, s: (i + v[1], 0, 0))

    prod_spec = pl.BlockSpec((chan, BLOCK, wide), lambda i, s: (0, i, 0))
    out_spec = pl.BlockSpec((BLOCK, own, chan), lambda i, s: (i, 0, 0))
    pad = small[-1].shape[0]
    return pl.pallas_call(
        behind(update_kernel, 7 + len(small), after),
        grid_spec=pltpu.PrefetchScalarGridSpec(
            num_scalar_prefetch=1,
            grid=(half // BLOCK,),
            in_specs=[prod_spec, prod_spec, kept(low), kept(high), got(low_got), got(high_got)]
            + [full_block(*v.shape) for v in small]
            + [ANYWHERE] * len(after),
            out_specs=[
                out_spec,
                out_spec,
                pl.BlockSpec((heads, BLOCK, wide), lambda i, s: (0, i, 0)),
            ],
            scratch_shapes=[
                pltpu.VMEM((chan * BLOCK, wide), F32),
                pltpu.VMEM((pad * BLOCK, wide), F32),
                pltpu.VMEM((chan, BLOCK * wide), BF16),
                pltpu.VMEM((chan, BLOCK * wide), BF16),
                pltpu.VMEM((chan, BLOCK * wide), F32),
            ],
        ),
        out_shape=[
            jax.ShapeDtypeStruct((half, own, chan), BF16),
            jax.ShapeDtypeStruct((half, own, chan), BF16),
            jax.ShapeDtypeStruct((heads, half, wide), BF16),
        ],
        compiler_params=pltpu.CompilerParams(vmem_limit_bytes=VMEM),
        cost_estimate=COST,
    )(scalars, prod, prod_got, low[0], high[0], low_got[0], high_got[0], *small, *after)


def table_kernel(origin, sizes, heads, count, scalars, *refs):
    group, table = refs[:4], refs[-1]
    late = len(refs) == 6
    wide = count // 2
    own = wide // 2
    length = scalars[0]
    pairs = [pl.program_id(0)] if late else range(2)
    for pair in pairs:
        first, start = origin + pair * wide, 0
        for size in sizes:
            half = size // 2
            for side in range(2):
                base = (first + side * half) % count
                spot = lax.broadcasted_iota(jnp.int32, (half, wide), 0)
                spot = spot + (scalars[3 + base // own] * own + base % own)
                masked = jnp.where(spot < length, 0.0, -1e9 * LOG2E)
                for h in range(heads):
                    parts = []
                    for j in range(2):
                        source = scalars[16 + 2 * pair + j]
                        value = group[0][h, start : start + half, :].astype(F32)
                        for d in range(1, 4):
                            other = group[d][h, start : start + half, :].astype(F32)
                            value = jnp.where(source == d, other, value)
                        parts.append(value[:, side * own : (side + 1) * own])
                    value = jnp.concatenate(parts, axis=1) * LOG2E + masked
                    if late:
                        table[h, side * half : (side + 1) * half, :] = value
                    else:
                        table[h, base : base + half, pair * wide : (pair + 1) * wide] = value
            start += half
            first += size


def bias_table(group, sizes, origin, table, scalars, heads, count):
    rest = [] if table is None else [table]
    size, wide = sizes[0], count // 2
    block = full_block(heads, count, count)
    if rest:
        block = pl.BlockSpec(
            (heads, size, wide), lambda i, s: (0, (origin + i * wide) % count // size, i)
        )
    return pl.pallas_call(
        functools.partial(table_kernel, origin, sizes, heads, count),
        grid_spec=pltpu.PrefetchScalarGridSpec(
            num_scalar_prefetch=1,
            grid=(2 if rest else 1,),
            in_specs=[full_block(*v.shape) for v in group] + [ANYWHERE] * len(rest),
            out_specs=block,
        ),
        out_shape=jax.ShapeDtypeStruct((heads, count, count), F32),
        input_output_aliases={5: 0} if rest else {},
        compiler_params=pltpu.CompilerParams(vmem_limit_bytes=VMEM),
        cost_estimate=COST,
    )(scalars, *group, *rest)


def attention_kernel(parts, scalars, table, gain_ref, w_ref, wo_ref, *refs):
    pieces, outs = refs[:parts], refs[parts : parts + 4]
    work, result, keys, queries, values, gates, attended, scores_a, scores_b = refs[parts + 4 :]
    heads, count = table.shape[0], table.shape[1]
    chan = work.shape[1]
    own = count // 4
    depth = chan // heads
    first = 0
    for ref in pieces:
        size = ref.shape[0] * BLOCK
        work[first : first + size, :] = ref[...].astype(F32).reshape(size, chan)
        first += size

    def project(b, carry):
        normed = norm_columns(work[pl.ds(b, count, stride=BLOCK), :].T, gain_ref[...])
        every = jnp.dot(w_ref[...], normed, preferred_element_type=F32)
        queries[b] = (every[:chan] * (depth ** (-0.5) * LOG2E)).astype(BF16)
        keys[b] = every[chan : 2 * chan].astype(BF16).T
        values[b] = every[2 * chan : 3 * chan].astype(BF16)
        gates[b] = 0.5 * jnp.tanh(every[3 * chan :]) + 0.5
        return carry

    lax.fori_loop(0, BLOCK, project, 0, unroll=8)

    def score(b, out):
        for h in range(heads):
            alone = [queries[b, h * depth : (h + 1) * depth]]
            if h > 0:
                alone.insert(0, jnp.zeros((h * depth, count), BF16))
            if h < heads - 1:
                alone.append(jnp.zeros(((heads - 1 - h) * depth, count), BF16))
            alone = jnp.concatenate(alone, axis=0)
            out[h] = jnp.dot(keys[b], alone, preferred_element_type=F32) + table[h]

    def attend(b, scores):
        for h in range(heads):
            weights = jnp.exp2(scores[h] - jnp.max(scores[h], axis=0, keepdims=True))
            total = jnp.sum(weights, axis=0, keepdims=True)
            part = pl.ds(h * depth, depth)
            mixed = jnp.dot(values[b, part], weights.astype(BF16), preferred_element_type=F32)
            attended[b, part] = (mixed * (1.0 / total) * gates[b, part]).astype(BF16)

    score(0, scores_a)

    def two_columns(i, carry):
        b = 2 * i
        score(b + 1, scores_b)
        attend(b, scores_a)
        score(jnp.minimum(b + 2, BLOCK - 1), scores_a)
        attend(b + 1, scores_b)
        return carry

    lax.fori_loop(0, BLOCK // 2, two_columns, 0)

    def finish(b, carry):
        rows = pl.ds(b, count, stride=BLOCK)
        change = jnp.dot(wo_ref[...], attended[b], preferred_element_type=F32)
        result[rows, :] = work[rows, :] + change.T
        return carry

    lax.fori_loop(0, BLOCK, finish, 0, unroll=8)
    for d in range(4):
        rows = pl.ds(pl.multiple_of(scalars[21 + d] * (own * BLOCK), own * BLOCK), own * BLOCK)
        outs[d][...] = result[rows, :].reshape(own, BLOCK, chan).astype(BF16)


def attention(index, scalars, table, gain, w, wo, pieces):
    heads, count = table.shape[0], table.shape[1]
    own, chan = pieces[0].shape[1], pieces[0].shape[2]
    return pl.pallas_call(
        functools.partial(attention_kernel, len(pieces)),
        grid_spec=pltpu.PrefetchScalarGridSpec(
            num_scalar_prefetch=1,
            grid=(1,),
            in_specs=[full_block(*v.shape) for v in (table, gain, w, wo)]
            + [pl.BlockSpec((m.shape[0], BLOCK, chan), lambda i, s: (0, index, 0)) for m in pieces],
            out_specs=[full_block(own, BLOCK, chan)] * 4,
            scratch_shapes=[
                pltpu.VMEM((count * BLOCK, chan), F32),
                pltpu.VMEM((count * BLOCK, chan), F32),
                pltpu.VMEM((BLOCK, count, chan), BF16),
                pltpu.VMEM((BLOCK, chan, count), BF16),
                pltpu.VMEM((BLOCK, chan, count), BF16),
                pltpu.VMEM((BLOCK, chan, count), F32),
                pltpu.VMEM((BLOCK, chan, count), BF16),
                pltpu.VMEM((heads, count, count), F32),
                pltpu.VMEM((heads, count, count), F32),
            ],
        ),
        out_shape=[jax.ShapeDtypeStruct((own, BLOCK, chan), BF16)] * 4,
        compiler_params=pltpu.CompilerParams(vmem_limit_bytes=VMEM),
        cost_estimate=COST,
    )(scalars, table, gain, w, wo, *pieces)


def place_kernel(index, scalars, *refs):
    output, sems = refs[-2:]
    copies = []
    for d in range(4):
        own = refs[d].shape[0]
        first = pl.multiple_of(scalars[25 + d] * own + index * BLOCK, BLOCK)
        copies.append(
            pltpu.make_async_copy(refs[d], output.at[:, pl.ds(first, BLOCK), :], sems.at[d])
        )
    for copy in copies:
        copy.start()
    for copy in copies:
        copy.wait()


def place(got, output, index, scalars):
    own, _, chan = got[0].shape
    rest = [] if output is None else [output]
    return pl.pallas_call(
        functools.partial(place_kernel, index),
        grid_spec=pltpu.PrefetchScalarGridSpec(
            num_scalar_prefetch=1,
            grid=(1,),
            in_specs=[full_block(*v.shape) for v in got] + [ANYWHERE] * len(rest),
            out_specs=ANYWHERE,
            scratch_shapes=[pltpu.SemaphoreType.DMA((4,))],
        ),
        out_shape=jax.ShapeDtypeStruct((own, 4 * own, chan), BF16),
        input_output_aliases={5: 0} if rest else {},
        cost_estimate=COST,
    )(scalars, *got, *rest)


def line_body(
    pair, lengths, gain_in, tri_in, tri_gate, gain_mid, tri_out, gain_att, att_in, att_bias, att_out
):
    own_rows = pair[0]
    own, count, chan = own_rows.shape
    heads = att_bias.shape[1]
    half = own // 2
    z = lax.axis_index("wide")
    inner = jnp.where(z < 2, 1, 2)
    partner = inner ^ 1
    other_in = 3 - inner
    other_out = other_in ^ 1
    order = jnp.stack([inner, partner, other_in, other_out])
    outer = ((z == 0) | (z == 3)).astype(jnp.int32)
    firsts = order * own
    scalars = jnp.concatenate(
        [
            lengths[:1],
            jnp.stack([inner, partner]),
            order,
            jnp.stack([outer]),
            firsts,
            firsts + half,
            (z - order) % 4,
            jnp.stack([z]),
            jnp.stack([jnp.argmax(order == (z + d) % 4) for d in range(4)]),
            (z - jnp.arange(4)) % 4,
            jnp.stack([z * own]),
        ]
    ).astype(jnp.int32)

    to_inner = [(0, 1), (3, 2)]
    to_outer = [(1, 0), (2, 3)]
    middle_link = [(1, 2), (2, 1)]

    def send(v, pairs):
        return lax.ppermute(v, "wide", pairs)

    def column(v):
        return v.reshape(chan, 1)

    tri_w = (jnp.swapaxes(tri_in, 1, 2).astype(F32) * 0.5).astype(BF16).reshape(4 * chan, chan)
    gain = column(gain_in)

    oi_rows = send(own_rows, middle_link)
    p_halves = [send(v, to_inner) for v in (own_rows[:half], own_rows[half:])]
    left_own, right_own, own_cut, p_got = operands(own_rows, scalars, 29, gain, tri_w, 2, (2, 20))
    own_got = send(own_cut, to_outer)
    p_a = tie(p_halves[0], left_own)
    left_pa, right_pa = operands(p_a, scalars, 9, gain, tri_w, 2, ())
    oi_rows = tie(oi_rows, left_pa)
    p_a = tie(p_a, oi_rows)
    left_oi, oi_cut = operands(oi_rows, scalars, 10, gain, tri_w, 1, (2,))
    oi_got = send(oi_cut, to_outer)
    p_b = tie(p_halves[1], left_oi, own_got)
    oo_halves = [send(v, middle_link) for v in (p_a, p_b)]

    bias_w = jnp.zeros((8, chan), BF16).at[:heads].set(att_bias.T)
    small = [
        gain,
        column(gain_mid),
        column(gain_att),
        (tri_out.astype(F32) * 0.5).astype(BF16).T,
        (tri_gate.astype(F32) * 0.5).astype(BF16).T,
        bias_w,
    ]
    near, far = half // BLOCK, half // (2 * BLOCK)
    pieces, biases = [], []

    left_pb, right_pb = operands(p_b, scalars, 13, gain, tri_w, 2, ())
    rights = [right_own, right_pa, right_pb]
    kept_own, sent_own, kept_p, _ = products([[left_own], [left_pa, left_pb]], rights)
    left_a, a_cut = operands(oo_halves[0], scalars, 11, gain, tri_w, 1, (2,), kept_p, oi_got)
    a_got = send(a_cut, to_outer)
    kept_oi, sent_oi, kept_a, sent_a = products([[left_oi], [left_a]], rights)

    def update(kept, got, low, high, low_got, high_got, *after):
        low, high, bias = updates(
            kept, got, low, high, low_got, high_got, scalars, small, heads, *after
        )
        pieces.extend([low, high])
        biases.append(bias)
        return bias

    def gather(members):
        joined = members[0] if len(members) == 1 else jnp.concatenate(members, axis=1)
        return [joined] + [
            send(joined, [(i, (i + d) % 4) for i in range(4)]) for d in range(1, 4)
        ]

    last = update(
        kept_own, send(sent_own, to_outer), (own_rows, 0), (own_rows, near), (own_got, 0), (own_got, near), kept_oi
    )
    last = update(kept_p, kept_own, (p_a, 0), (p_b, 0), (p_got, 0), (p_got, near), last)
    left_b, b_cut = operands(oo_halves[1], scalars, 15, gain, tri_w, 1, (2,), last)
    b_got = send(b_cut, to_outer)
    kept_b, sent_b = products([[left_b]], rights)
    last = update(
        kept_oi, send(sent_oi, to_outer), (oi_rows, 0), (oi_rows, near), (oi_got, 0), (oi_got, near), kept_b
    )
    low = oo_halves[0]
    last = update(kept_a, send(sent_a, to_outer), (low, 0), (low, far), (a_got, 0), (a_got, far), last)
    early = [own, own, own, half]
    table = bias_table(gather(biases), early, 0, None, scalars, heads, count)
    low = oo_halves[1]
    last = update(kept_b, send(sent_b, to_outer), (low, 0), (low, far), (b_got, 0), (b_got, far), table)
    table = bias_table(gather([last]), [half], sum(early), table, scalars, heads, count)

    att_w = jnp.swapaxes(att_in, 1, 2).astype(F32) * jnp.array([1, 1, 1, 0.5], F32).reshape(4, 1, 1)
    att_w = att_w.astype(BF16).reshape(4 * chan, chan)
    output = None
    for index in range(own // BLOCK):
        got = list(attention(index, scalars, table, column(gain_att), att_w, att_out.T, pieces))
        for d in range(1, 4):
            got[d] = send(got[d], [(i, (i + d) % 4) for i in range(4)])
        output = place(got, output, index, scalars)
    return output[None]


def solution(mesh):
    in_specs = (
        P(("groups", "dp"), "wide", None, None),
        P(("groups", "dp")),
        P(),
        P(),
        P(),
        P(),
        P(),
        P(),
        P(),
        P(),
        P(),
    )
    out_specs = P(("groups", "dp"), "wide", None, None)
    body = line_body if mesh.shape["wide"] == 4 else general_body
    return jax.shard_map(body, mesh=mesh, in_specs=in_specs, out_specs=out_specs, check_vma=False)
```
